32 devices in a mesh: ctx: 8 (over z, y), tp: 4 (over x, core).
Axes of the slice: x: 2, y: 2, z: 4, core: 2. Of those that a mesh axis runs over, the one named last changes fastest.
Arguments:
- query_proj: bfloat16 [1024, 4096], P('ctx', 'tp'), may hold values from -6 to 6
- key_proj: bfloat16 [1024, 4096], P('ctx', 'tp'), may hold values from -6 to 6
- value_proj: bfloat16 [1024, 4096], P('ctx', 'tp'), may hold values from -6 to 6
- filters: float32 [256, 128], P('tp'), may hold values from -0.5 to 0.5
- skip_gain: float32 [4096], P('tp'), may hold values from -1 to 1
- out_grad: bfloat16 [1024, 4096], P('ctx', 'tp'), may hold values from -6 to 6
- w_out: bfloat16 [4096, 4096], P('tp'), may hold values from -0.09375 to 0.09375
Outputs:
- query_grad: bfloat16 [1024, 4096], P('ctx', 'tp')
- key_grad: bfloat16 [1024, 4096], P('ctx', 'tp')
- value_grad: bfloat16 [1024, 4096], P('ctx', 'tp')
- filter_grad: float32 [256, 128], P('tp')
- skip_grad: float32 [4096], P('tp')
The draws below stay inside these ranges and needn't reach their ends.
All inputs are finite; a program needn't handle non-finite values.
Results may differ from the reference program's by a relative error of at most 0.0075.
Values may be sent and summed in bfloat16 or wider, within the bound.
A program may use at most 128 MiB of HBM per device.

```python
import jax
import jax.numpy as jnp
from jax import lax

D = 4096
KLEN = 128
TOKENS = 1024
GROUPS = 256


def levels(key, extent, split, low, largest):
    level, own = 1.0, jax.random.fold_in(key, 6)
    for position, shards_of in split:
        draws = jnp.exp(jax.random.uniform(jax.random.fold_in(own, position), (shards_of,), jnp.float32, low / len(split), largest / len(split)))
        level = level * jnp.repeat(draws, extent[position] // shards_of).reshape([-1 if axis == position else 1 for axis in range(len(extent))])
    return level


def centred(stream_key, shape, deviation, reach, split=(), held_as=jnp.bfloat16):
    array = jax.random.normal(stream_key, shape, jnp.float32) * deviation
    if len(split) > 0:
        array = levels(stream_key, shape, split, -0.22, 0.18) * array
    return jnp.clip(array, min=-reach, max=reach).astype(held_as)


def setup_inputs(seed: int = 0) -> dict:
    key_list = jax.random.split(jax.random.key(seed), 8)
    query_proj = centred(key_list[0], (TOKENS, D), 1.0, 6.0, ((0, 8), (1, 4)))
    key_proj = centred(key_list[1], (TOKENS, D), 1.0, 6.0, ((0, 8), (1, 4)))
    value_proj = centred(key_list[2], (TOKENS, D), 1.0, 6.0, ((0, 8), (1, 4)))
    filters = centred(key_list[3], (GROUPS, KLEN), KLEN ** -0.5, 0.5, ((0, 4),), jnp.float32)
    skip_gain = jnp.clip(jax.random.uniform(key_list[4], (D,), jnp.float32, -1.0, 1.0) * levels(key_list[4], (D,), ((0, 4),), -0.4, 0.0), -1.0, 1.0)
    out_grad = centred(key_list[5], (TOKENS, D), 1.0, 6.0, ((0, 8), (1, 4)))
    w_out = centred(key_list[6], (D, D), D ** -0.5, 0.09375, ((0, 4),))
    return dict(query_proj=query_proj, key_proj=key_proj, value_proj=value_proj, filters=filters, skip_gain=skip_gain, out_grad=out_grad, w_out=w_out)


def blocks_of(extended, width):
    count = (extended.shape[0] - width) // width
    channels = extended.shape[1]
    first = extended[:-width].reshape(count, width, channels)
    second = extended[width:].reshape(count, width, channels)
    return jnp.concatenate([first, second], axis=1)


def tap_table(filters, causal):
    width = filters.shape[1]
    rows = jnp.arange(width)[:, None]
    cols = jnp.arange(2 * width)[None, :]
    lag = rows + width - cols if causal else cols - rows
    valid = (lag >= 0) & (lag < width)
    index = jnp.clip(lag, 0, width - 1).astype(jnp.int32)
    table = filters[:, index]
    return jnp.where(valid[None], table, jnp.float32(0.0))


def convolve(extended, filters, skip_gain, causal):
    width = filters.shape[1]
    groups = filters.shape[0]
    channels = extended.shape[1]
    window = blocks_of(extended, width)
    count = window.shape[0]
    window = window.reshape(count, 2 * width, groups, channels // groups)
    mixed = jnp.einsum('gij,bjgc->bigc', tap_table(filters, causal), window, precision=lax.Precision.HIGHEST)
    mixed = mixed.reshape(count * width, channels)
    current = extended[width:] if causal else extended[:-width]
    return mixed + skip_gain[None, :] * current


def reference(query_proj, key_proj, value_proj, filters, skip_gain, out_grad, w_out):
    width = filters.shape[1]
    groups = filters.shape[0]
    channels = query_proj.shape[1]
    query_f = query_proj.astype(jnp.float32)
    key_f = key_proj.astype(jnp.float32)
    value_f = value_proj.astype(jnp.float32)
    products = (key_f * value_f).astype(jnp.bfloat16)
    product_f = products.astype(jnp.float32)
    mixer_grad = lax.dot_general(out_grad, w_out, (((1,), (1,)), ((), ())), preferred_element_type=jnp.float32)
    padding = jnp.zeros((width, channels), jnp.float32)
    prod_ext = jnp.concatenate([padding, product_f], axis=0)
    filtered = convolve(prod_ext, filters, skip_gain, True)
    query_grad = (mixer_grad * filtered).astype(jnp.bfloat16)
    filtered_grad = (mixer_grad * query_f).astype(jnp.bfloat16)
    grad_f = filtered_grad.astype(jnp.float32)
    grad_ext = jnp.concatenate([grad_f, padding], axis=0)
    product_grad = convolve(grad_ext, filters, skip_gain, False)
    key_grad = (product_grad * value_f).astype(jnp.bfloat16)
    value_grad = (product_grad * key_f).astype(jnp.bfloat16)
    window = blocks_of(prod_ext, width)
    count = window.shape[0]
    window = window.reshape(count, 2 * width, groups, channels // groups)
    grad_blocks = grad_f.reshape(count, width, groups, channels // groups)
    pairs = jnp.einsum('bigc,bjgc->gij', grad_blocks, window, precision=lax.Precision.HIGHEST)
    rows = jnp.arange(width)[:, None, None]
    cols = jnp.arange(2 * width)[None, :, None]
    lags = jnp.arange(width)[None, None, :]
    picker = (cols == rows + width - lags).astype(jnp.float32)
    filter_grad = jnp.einsum('gij,ijl->gl', pairs, picker, precision=lax.Precision.HIGHEST)
    skip_grad = jnp.sum(grad_f * product_f, axis=0)
    return (query_grad, key_grad, value_grad, filter_grad, skip_grad)
```

```python
import functools

import jax
import jax.numpy as jnp
from jax import lax
from jax.experimental import pallas as pl
from jax.experimental.pallas import tpu as pltpu
from jax.sharding import PartitionSpec as P

MESH = pl.DeviceIdType.MESH
LANES = 128
NT = (((1,), (1,)), ((), ()))
PIECES = 2


def kernel(
    n_ctx, n_tp,
    q_ref, k_ref, v_ref, f_ref, s_ref, og_ref, w_hbm,
    qg_ref, kg_ref, vg_ref, fg_ref, sg_ref,
    wv, ogb, x, xp, g, gn, a1, b1, a2, b2, mg, filt, part, rsb, red,
    w_sem, og_send, og_recv, fw_send, x_send, x_recv, g_send, g_recv,
    rs_send, rs_recv, ag_send, ag_recv,
):
    rows, channels = q_ref.shape
    tiles = channels // LANES
    per_tile = f_ref.shape[0] // tiles
    span = LANES // per_tile
    wide = channels // PIECES
    step = n_ctx // tiles
    me = lax.axis_index("ctx")
    tp = lax.axis_index("tp")
    mate = tp + 1 - 2 * lax.rem(tp, 2)
    across = [lax.rem(tp + 2 * d, n_tp) for d in range(1, n_tp // 2)]
    across_mate = [a + 1 - 2 * lax.rem(a, 2) for a in across]
    order = [tp, mate] + across + across_mate

    w_copies = []
    for n, slot in enumerate(order):
        copy = pltpu.make_async_copy(
            w_hbm.at[:, pl.ds(pl.multiple_of(slot * channels, channels), channels)], wv.at[n], w_sem.at[n]
        )
        copy.start()
        w_copies.append(copy)

    barrier = pltpu.get_barrier_semaphore()
    for peer in order[1:]:
        pl.semaphore_signal(barrier, inc=1, device_id=(me, peer), device_id_type=MESH)

    @pl.loop(1, n_ctx)
    def _(d):
        pl.semaphore_signal(barrier, inc=1, device_id=(lax.rem(me + d, n_ctx), tp), device_id_type=MESH)

    @pl.loop(0, tiles)
    def _(i):
        cols = pl.ds(pl.multiple_of(i * LANES, LANES), LANES)
        x[i] = (k_ref[:, cols].astype(jnp.float32) * v_ref[:, cols].astype(jnp.float32)).astype(jnp.bfloat16)

    pl.semaphore_wait(barrier, n_tp - 1 + n_ctx - 1)

    def og_copy(p, n, peer):
        return pltpu.make_async_remote_copy(
            src_ref=og_ref.at[:, pl.ds(p * wide, wide)], dst_ref=ogb.at[tp, p],
            send_sem=og_send.at[n, p], recv_sem=og_recv.at[tp, p],
            device_id=(me, peer), device_id_type=MESH,
        )

    def forward_copy(slot, p, n):
        return pltpu.make_async_remote_copy(
            src_ref=ogb.at[slot, p], dst_ref=ogb.at[slot, p],
            send_sem=fw_send.at[n, p], recv_sem=og_recv.at[slot, p],
            device_id=(me, mate), device_id_type=MESH,
        )

    direct = across + [mate]
    for p in range(PIECES):
        for n, peer in enumerate(direct):
            og_copy(p, n, peer).start()

    x_copy = pltpu.make_async_remote_copy(
        src_ref=x, dst_ref=xp, send_sem=x_send, recv_sem=x_recv,
        device_id=(lax.rem(me + 1, n_ctx), tp), device_id_type=MESH,
    )

    @pl.when(me < n_ctx - 1)
    def _():
        x_copy.start()

    row = lax.broadcasted_iota(jnp.int32, (rows, LANES), 0)
    col = lax.broadcasted_iota(jnp.int32, (rows, LANES), 1)
    mirror = jnp.where(lax.rem(row + col, LANES) == 0, 1.0, 0.0).astype(jnp.bfloat16)

    def spread(line):
        return pltpu.roll(jnp.broadcast_to(line, (rows, LANES)), 0, 1, stride=1, stride_axis=0)

    @pl.loop(0, tiles)
    def _(i):
        taps = f_ref[pl.ds(pl.multiple_of(i * per_tile, per_tile), per_tile), :]
        back = jnp.dot(taps.astype(jnp.bfloat16), mirror, preferred_element_type=jnp.float32)
        for j in range(per_tile):
            at = pl.ds(j * LANES, LANES)
            c1 = spread(back[j : j + 1])
            a1[i, :, at] = jnp.where(col > row, c1, 0.0).astype(jnp.bfloat16)
            b1[i, :, at] = jnp.where(col <= row, c1, 0.0).astype(jnp.bfloat16)
            c2 = spread(taps[j : j + 1])
            a2[i, :, at] = jnp.where(col < row, c2, 0.0).astype(jnp.bfloat16)
            b2[i, :, at] = jnp.where(col >= row, c2, 0.0).astype(jnp.bfloat16)

    lane = lax.broadcasted_iota(jnp.int32, (1, LANES), 1)
    masks = [
        jnp.where((lane >= j * span) & (lane < (j + 1) * span), 1.0, 0.0).astype(jnp.bfloat16)
        for j in range(per_tile)
    ]

    def by_group(block):
        return jnp.concatenate([block * m for m in masks], axis=0)

    def project(n, block_of, first):
        @pl.loop(0, tiles // 2)
        def _(i):
            chans = pl.ds(pl.multiple_of(i * 2 * LANES, 2 * LANES), 2 * LANES)
            total = None
            for p in range(PIECES):
                term = lax.dot_general(
                    block_of(p), wv[n, chans, pl.ds(p * wide, wide)], NT, preferred_element_type=jnp.float32
                )
                total = term if total is None else total + term
            if first:
                mg[:, chans] = total
            else:
                mg[:, chans] += total

    w_copies[0].wait()
    project(0, lambda p: og_ref[:, pl.ds(p * wide, wide)], True)

    for p in range(PIECES):
        forward_copy(mate, p, 0).wait_recv()
    w_copies[1].wait()
    project(1, lambda p: ogb[mate, p], False)

    @pl.when(me > 0)
    def _():
        x_copy.wait_recv()

    @pl.when(me == 0)
    def _():
        xp[...] = jnp.zeros_like(xp)

    for p in range(PIECES):
        for n, a in enumerate(across):
            forward_copy(a, p, n).wait_recv()
            forward_copy(a, p, n).start()

    @pl.loop(0, tiles)
    def _(i):
        cols = pl.ds(pl.multiple_of(i * LANES, LANES), LANES)
        y = jnp.dot(a1[i], by_group(xp[i]), preferred_element_type=jnp.float32)
        y += jnp.dot(b1[i], by_group(x[i]), preferred_element_type=jnp.float32)
        filt[:, cols] = y + s_ref[:, cols] * x[i].astype(jnp.float32)

    for n, a in enumerate(across):
        w_copies[2 + n].wait()
        project(2 + n, lambda p, a=a: ogb[a, p], False)
    for n, a in enumerate(across_mate):
        for p in range(PIECES):
            forward_copy(a, p, n).wait_recv()
        w_copies[2 + len(across) + n].wait()
        project(2 + len(across) + n, lambda p, a=a: ogb[a, p], False)

    def g_copy(i):
        return pltpu.make_async_remote_copy(
            src_ref=g.at[i], dst_ref=gn.at[i], send_sem=g_send.at[i], recv_sem=g_recv.at[i],
            device_id=(lax.rem(me + n_ctx - 1, n_ctx), tp), device_id_type=MESH,
        )

    @pl.loop(0, tiles)
    def _(i):
        cols = pl.ds(pl.multiple_of(i * LANES, LANES), LANES)
        m = mg[:, cols]
        g[i] = (m * q_ref[:, cols].astype(jnp.float32)).astype(jnp.bfloat16)

        @pl.when(me > 0)
        def _():
            g_copy(i).start()

        qg_ref[:, cols] = (m * filt[:, cols]).astype(jnp.bfloat16)

    flip = jnp.where(row + col == rows - 1, 1.0, 0.0).astype(jnp.bfloat16)

    def upside_down(block):
        return jnp.dot(flip, block, preferred_element_type=jnp.float32).astype(jnp.bfloat16)

    @pl.loop(0, tiles)
    def _(i):
        gt = g[i]
        far = lax.dot_general(by_group(upside_down(xp[i])), gt, NT, preferred_element_type=jnp.float32)
        near = lax.dot_general(by_group(upside_down(x[i])), gt, NT, preferred_element_type=jnp.float32)
        for j in range(per_tile):
            at = slice(j * rows, (j + 1) * rows)
            pairs = jnp.where(col + row >= rows - 1, near[at], far[at])
            turned = pltpu.roll(pairs, 0, 1, stride=1, stride_axis=0)
            part[i, pl.ds(j, 1), :] = jnp.sum(turned, axis=0, keepdims=True)
        part[i, pl.ds(0, per_tile), :] = pltpu.roll(part[i, pl.ds(0, per_tile), :], 1, 1)
        both = gt.astype(jnp.float32) * x[i].astype(jnp.float32)
        part[i, pl.ds(per_tile, 8), :] = jnp.sum(both.reshape(rows // 8, 8, LANES), axis=0)

    def rs_copy(i):
        return pltpu.make_async_remote_copy(
            src_ref=part.at[i], dst_ref=rsb.at[me], send_sem=rs_send.at[i], recv_sem=rs_recv.at[me],
            device_id=(i * step, tp), device_id_type=MESH,
        )

    def rs_arrival(d):
        source = lax.rem(me + d, n_ctx)
        return source, pltpu.make_async_remote_copy(
            src_ref=part.at[0], dst_ref=rsb.at[source], send_sem=rs_send.at[0], recv_sem=rs_recv.at[source],
            device_id=(source, tp), device_id_type=MESH,
        )

    mine = me // step
    owner = lax.rem(me, step) == 0

    @pl.loop(0, tiles)
    def _(i):
        @pl.when(i * step != me)
        def _():
            rs_copy(i).start()

    @pl.loop(0, tiles)
    def _(i):
        cols = pl.ds(pl.multiple_of(i * LANES, LANES), LANES)
        z = jnp.dot(b2[i], by_group(g[i]), preferred_element_type=jnp.float32)
        mg[:, cols] = z + s_ref[:, cols] * g[i].astype(jnp.float32)

    def ag_copy(d):
        return pltpu.make_async_remote_copy(
            src_ref=red.at[mine], dst_ref=red.at[mine], send_sem=ag_send.at[d], recv_sem=ag_recv.at[mine],
            device_id=(lax.rem(me + d, n_ctx), tp), device_id_type=MESH,
        )

    def ag_arrival(i):
        return pltpu.make_async_remote_copy(
            src_ref=red.at[i], dst_ref=red.at[i], send_sem=ag_send.at[0], recv_sem=ag_recv.at[i],
            device_id=(i * step, tp), device_id_type=MESH,
        )

    @pl.when(owner)
    def _():
        def gather(d, total):
            source, arrival = rs_arrival(d)
            arrival.wait_recv()
            return total + rsb[source]

        red[mine] = lax.fori_loop(1, n_ctx, gather, part[mine])

        @pl.loop(1, n_ctx)
        def _(d):
            ag_copy(d).start()

    @pl.loop(0, tiles)
    def _(i):
        cols = pl.ds(pl.multiple_of(i * LANES, LANES), LANES)

        @pl.when(me < n_ctx - 1)
        def _():
            g_copy(i).wait_recv()
            mg[:, cols] += jnp.dot(a2[i], by_group(gn[i]), preferred_element_type=jnp.float32)

        z = mg[:, cols]
        kg_ref[:, cols] = (z * v_ref[:, cols].astype(jnp.float32)).astype(jnp.bfloat16)
        vg_ref[:, cols] = (z * k_ref[:, cols].astype(jnp.float32)).astype(jnp.bfloat16)

    for i in range(tiles):
        @pl.when(i * step != me)
        def _():
            ag_arrival(i).wait_recv()

        fg_ref[pl.ds(i * per_tile, per_tile), :] = red[i, pl.ds(0, per_tile), :]
        sg_ref[:, pl.ds(i * LANES, LANES)] = jnp.sum(red[i, pl.ds(per_tile, 8), :], axis=0, keepdims=True)

    for p in range(PIECES):
        for n, peer in enumerate(direct):
            og_copy(p, n, peer).wait_send()
        for n, a in enumerate(across):
            forward_copy(a, p, n).wait_send()

    @pl.when(me < n_ctx - 1)
    def _():
        x_copy.wait_send()

    @pl.when(me > 0)
    def _():
        @pl.loop(0, tiles)
        def _(i):
            g_copy(i).wait_send()

    @pl.loop(0, tiles)
    def _(i):
        @pl.when(i * step != me)
        def _():
            rs_copy(i).wait_send()

    @pl.when(owner)
    def _():
        @pl.loop(1, n_ctx)
        def _(d):
            ag_copy(d).wait_send()


def on_device(n_ctx, n_tp, q, k, v, filters, skip_gain, out_grad, w_out):
    rows, channels = q.shape
    tiles = channels // LANES
    groups = filters.shape[0]
    block = (groups // tiles) + 8
    vmem = pl.BlockSpec(memory_space=pltpu.VMEM)
    bf, fl = jnp.bfloat16, jnp.float32
    dma = pltpu.SemaphoreType.DMA
    table = pltpu.VMEM((tiles, rows, (groups // tiles) * LANES), bf)
    slab = pltpu.VMEM((tiles, rows, LANES), bf)
    out = pl.pallas_call(
        functools.partial(kernel, n_ctx, n_tp),
        out_shape=(
            jax.ShapeDtypeStruct((rows, channels), bf),
            jax.ShapeDtypeStruct((rows, channels), bf),
            jax.ShapeDtypeStruct((rows, channels), bf),
            jax.ShapeDtypeStruct(filters.shape, fl),
            jax.ShapeDtypeStruct((1, channels), fl),
        ),
        in_specs=[vmem] * 6 + [pl.BlockSpec(memory_space=pl.ANY)],
        out_specs=(vmem,) * 5,
        scratch_shapes=[
            pltpu.VMEM((n_tp, channels, channels), bf),
            pltpu.VMEM((n_tp, PIECES, rows, channels // PIECES), bf),
            slab, slab, slab, slab,
            table, table, table, table,
            pltpu.VMEM((rows, channels), fl),
            pltpu.VMEM((rows, channels), fl),
            pltpu.VMEM((tiles, block, LANES), fl),
            pltpu.VMEM((n_ctx, block, LANES), fl),
            pltpu.VMEM((tiles, block, LANES), fl),
            dma((n_tp,)),
            dma((n_tp // 2, PIECES)),
            dma((n_tp, PIECES)),
            dma((n_tp // 2, PIECES)),
            dma, dma,
            dma((tiles,)), dma((tiles,)),
            dma((tiles,)), dma((n_ctx,)),
            dma((n_ctx,)), dma((tiles,)),
        ],
        compiler_params=pltpu.CompilerParams(
            collective_id=0, has_side_effects=True, vmem_limit_bytes=48 * 1024 * 1024
        ),
        cost_estimate=pl.CostEstimate(
            flops=2 * rows * channels * channels * n_tp, bytes_accessed=2 * channels * channels * n_tp, transcendentals=0
        ),
    )(q, k, v, filters, skip_gain.reshape(1, channels), out_grad, w_out)
    return out[:4] + (out[4].reshape(channels),)


def solution(mesh):
    n_ctx, n_tp = mesh.shape["ctx"], mesh.shape["tp"]
    return jax.shard_map(
        functools.partial(on_device, n_ctx, n_tp),
        mesh=mesh,
        in_specs=(
            P("ctx", "tp"),
            P("ctx", "tp"),
            P("ctx", "tp"),
            P("tp", None),
            P("tp"),
            P("ctx", "tp"),
            P("tp", None),
        ),
        out_specs=(P("ctx", "tp"), P("ctx", "tp"), P("ctx", "tp"), P("tp", None), P("tp")),
        check_vma=False,
    )
```

```python
import functools

import jax
import jax.numpy as jnp
from jax import lax
from jax.experimental import pallas as pl
from jax.experimental.pallas import tpu as pltpu
from jax.sharding import PartitionSpec as P

MESH = pl.DeviceIdType.MESH
LANES = 128
NT = (((1,), (1,)), ((), ()))
PIECES = 2


def kernel(
    n_ctx, n_tp,
    q_hbm, k_hbm, v_hbm, f_hbm, s_hbm, og_hbm, w_hbm,
    qg_ref, kg_ref, vg_ref, fg_ref, sg_ref,
    q_ref, k_ref, v_ref, f_ref, s_ref, og_ref, in_sem,
    wv, ogb, x, xp, g, gn, a1, b1, a2, b2, mg, filt, part, rsb, red,
    w_sem, og_send, og_recv, fw_send, x_send, x_recv, g_send, g_recv,
    rs_send, rs_recv, ag_send, ag_recv,
):
    rows, channels = q_ref.shape
    tiles = channels // LANES
    per_tile = f_ref.shape[0] // tiles
    span = LANES // per_tile
    wide = channels // PIECES
    step = n_ctx // tiles
    me = lax.axis_index("ctx")
    tp = lax.axis_index("tp")
    mate = tp + 1 - 2 * lax.rem(tp, 2)
    across = [lax.rem(tp + 2 * d, n_tp) for d in range(1, n_tp // 2)]
    across_mate = [a + 1 - 2 * lax.rem(a, 2) for a in across]
    order = [tp, mate] + across + across_mate

    def bring(n, source, target):
        copy = pltpu.make_async_copy(source, target, in_sem.at[n])
        copy.start()
        return copy

    k_in = bring(0, k_hbm, k_ref)
    v_in = bring(1, v_hbm, v_ref)
    og_in = bring(2, og_hbm, og_ref)
    f_in = bring(3, f_hbm, f_ref)
    s_in = bring(4, s_hbm, s_ref)
    q_in = bring(5, q_hbm, q_ref)

    w_copies = []
    for n, slot in enumerate(order):
        copy = pltpu.make_async_copy(
            w_hbm.at[:, pl.ds(pl.multiple_of(slot * channels, channels), channels)], wv.at[n], w_sem.at[n]
        )
        copy.start()
        w_copies.append(copy)

    barrier = pltpu.get_barrier_semaphore()
    for peer in order[1:]:
        pl.semaphore_signal(barrier, inc=1, device_id=(me, peer), device_id_type=MESH)

    @pl.loop(1, n_ctx)
    def _(d):
        pl.semaphore_signal(barrier, inc=1, device_id=(lax.rem(me + d, n_ctx), tp), device_id_type=MESH)

    k_in.wait()
    v_in.wait()

    @pl.loop(0, tiles)
    def _(i):
        cols = pl.ds(pl.multiple_of(i * LANES, LANES), LANES)
        x[i] = (k_ref[:, cols].astype(jnp.float32) * v_ref[:, cols].astype(jnp.float32)).astype(jnp.bfloat16)

    og_in.wait()
    pl.semaphore_wait(barrier, n_tp - 1 + n_ctx - 1)

    def og_copy(p, n, peer):
        return pltpu.make_async_remote_copy(
            src_ref=og_ref.at[:, pl.ds(p * wide, wide)], dst_ref=ogb.at[tp, p],
            send_sem=og_send.at[n, p], recv_sem=og_recv.at[tp, p],
            device_id=(me, peer), device_id_type=MESH,
        )

    def forward_copy(slot, p, n):
        return pltpu.make_async_remote_copy(
            src_ref=ogb.at[slot, p], dst_ref=ogb.at[slot, p],
            send_sem=fw_send.at[n, p], recv_sem=og_recv.at[slot, p],
            device_id=(me, mate), device_id_type=MESH,
        )

    direct = across + [mate]
    for p in range(PIECES):
        for n, peer in enumerate(direct):
            og_copy(p, n, peer).start()

    x_copy = pltpu.make_async_remote_copy(
        src_ref=x, dst_ref=xp, send_sem=x_send, recv_sem=x_recv,
        device_id=(lax.rem(me + 1, n_ctx), tp), device_id_type=MESH,
    )

    @pl.when(me < n_ctx - 1)
    def _():
        x_copy.start()

    f_in.wait()
    row = lax.broadcasted_iota(jnp.int32, (rows, LANES), 0)
    col = lax.broadcasted_iota(jnp.int32, (rows, LANES), 1)
    mirror = jnp.where(lax.rem(row + col, LANES) == 0, 1.0, 0.0).astype(jnp.bfloat16)

    def spread(line):
        return pltpu.roll(jnp.broadcast_to(line, (rows, LANES)), 0, 1, stride=1, stride_axis=0)

    @pl.loop(0, tiles)
    def _(i):
        taps = f_ref[pl.ds(pl.multiple_of(i * per_tile, per_tile), per_tile), :]
        back = jnp.dot(taps.astype(jnp.bfloat16), mirror, preferred_element_type=jnp.float32)
        for j in range(per_tile):
            at = pl.ds(j * LANES, LANES)
            c1 = spread(back[j : j + 1])
            a1[i, :, at] = jnp.where(col > row, c1, 0.0).astype(jnp.bfloat16)
            b1[i, :, at] = jnp.where(col <= row, c1, 0.0).astype(jnp.bfloat16)
            c2 = spread(taps[j : j + 1])
            a2[i, :, at] = jnp.where(col < row, c2, 0.0).astype(jnp.bfloat16)
            b2[i, :, at] = jnp.where(col >= row, c2, 0.0).astype(jnp.bfloat16)

    lane = lax.broadcasted_iota(jnp.int32, (1, LANES), 1)
    masks = [
        jnp.where((lane >= j * span) & (lane < (j + 1) * span), 1.0, 0.0).astype(jnp.bfloat16)
        for j in range(per_tile)
    ]

    def by_group(block):
        return jnp.concatenate([block * m for m in masks], axis=0)

    def project(n, block_of, first):
        @pl.loop(0, tiles // 2)
        def _(i):
            chans = pl.ds(pl.multiple_of(i * 2 * LANES, 2 * LANES), 2 * LANES)
            total = None
            for p in range(PIECES):
                term = lax.dot_general(
                    block_of(p), wv[n, chans, pl.ds(p * wide, wide)], NT, preferred_element_type=jnp.float32
                )
                total = term if total is None else total + term
            if first:
                mg[:, chans] = total
            else:
                mg[:, chans] += total

    w_copies[0].wait()
    project(0, lambda p: og_ref[:, pl.ds(p * wide, wide)], True)

    for p in range(PIECES):
        forward_copy(mate, p, 0).wait_recv()
    w_copies[1].wait()
    project(1, lambda p: ogb[mate, p], False)

    @pl.when(me > 0)
    def _():
        x_copy.wait_recv()

    @pl.when(me == 0)
    def _():
        xp[...] = jnp.zeros_like(xp)

    for p in range(PIECES):
        for n, a in enumerate(across):
            forward_copy(a, p, n).wait_recv()
            forward_copy(a, p, n).start()

    s_in.wait()

    @pl.loop(0, tiles)
    def _(i):
        cols = pl.ds(pl.multiple_of(i * LANES, LANES), LANES)
        y = jnp.dot(a1[i], by_group(xp[i]), preferred_element_type=jnp.float32)
        y += jnp.dot(b1[i], by_group(x[i]), preferred_element_type=jnp.float32)
        filt[:, cols] = y + s_ref[:, cols] * x[i].astype(jnp.float32)

    for n, a in enumerate(across):
        w_copies[2 + n].wait()
        project(2 + n, lambda p, a=a: ogb[a, p], False)
    for n, a in enumerate(across_mate):
        for p in range(PIECES):
            forward_copy(a, p, n).wait_recv()
        w_copies[2 + len(across) + n].wait()
        project(2 + len(across) + n, lambda p, a=a: ogb[a, p], False)

    q_in.wait()

    def g_copy(i):
        return pltpu.make_async_remote_copy(
            src_ref=g.at[i], dst_ref=gn.at[i], send_sem=g_send.at[i], recv_sem=g_recv.at[i],
            device_id=(lax.rem(me + n_ctx - 1, n_ctx), tp), device_id_type=MESH,
        )

    @pl.loop(0, tiles)
    def _(i):
        cols = pl.ds(pl.multiple_of(i * LANES, LANES), LANES)
        m = mg[:, cols]
        g[i] = (m * q_ref[:, cols].astype(jnp.float32)).astype(jnp.bfloat16)

        @pl.when(me > 0)
        def _():
            g_copy(i).start()

        qg_ref[:, cols] = (m * filt[:, cols]).astype(jnp.bfloat16)

    flip = jnp.where(row + col == rows - 1, 1.0, 0.0).astype(jnp.bfloat16)

    def upside_down(block):
        return jnp.dot(flip, block, preferred_element_type=jnp.float32).astype(jnp.bfloat16)

    @pl.loop(0, tiles)
    def _(i):
        gt = g[i]
        far = lax.dot_general(by_group(upside_down(xp[i])), gt, NT, preferred_element_type=jnp.float32)
        near = lax.dot_general(by_group(upside_down(x[i])), gt, NT, preferred_element_type=jnp.float32)
        for j in range(per_tile):
            at = slice(j * rows, (j + 1) * rows)
            pairs = jnp.where(col + row >= rows - 1, near[at], far[at])
            turned = pltpu.roll(pairs, 0, 1, stride=1, stride_axis=0)
            part[i, pl.ds(j, 1), :] = jnp.sum(turned, axis=0, keepdims=True)
        part[i, pl.ds(0, per_tile), :] = pltpu.roll(part[i, pl.ds(0, per_tile), :], 1, 1)
        both = gt.astype(jnp.float32) * x[i].astype(jnp.float32)
        part[i, pl.ds(per_tile, 8), :] = jnp.sum(both.reshape(rows // 8, 8, LANES), axis=0)

    def rs_copy(i):
        return pltpu.make_async_remote_copy(
            src_ref=part.at[i], dst_ref=rsb.at[me], send_sem=rs_send.at[i], recv_sem=rs_recv.at[me],
            device_id=(i * step, tp), device_id_type=MESH,
        )

    def rs_arrival(d):
        source = lax.rem(me + d, n_ctx)
        return source, pltpu.make_async_remote_copy(
            src_ref=part.at[0], dst_ref=rsb.at[source], send_sem=rs_send.at[0], recv_sem=rs_recv.at[source],
            device_id=(source, tp), device_id_type=MESH,
        )

    mine = me // step
    owner = lax.rem(me, step) == 0

    @pl.loop(0, tiles)
    def _(i):
        @pl.when(i * step != me)
        def _():
            rs_copy(i).start()

    @pl.loop(0, tiles)
    def _(i):
        cols = pl.ds(pl.multiple_of(i * LANES, LANES), LANES)
        z = jnp.dot(b2[i], by_group(g[i]), preferred_element_type=jnp.float32)
        mg[:, cols] = z + s_ref[:, cols] * g[i].astype(jnp.float32)

    def ag_copy(d):
        return pltpu.make_async_remote_copy(
            src_ref=red.at[mine], dst_ref=red.at[mine], send_sem=ag_send.at[d], recv_sem=ag_recv.at[mine],
            device_id=(lax.rem(me + d, n_ctx), tp), device_id_type=MESH,
        )

    def ag_arrival(i):
        return pltpu.make_async_remote_copy(
            src_ref=red.at[i], dst_ref=red.at[i], send_sem=ag_send.at[0], recv_sem=ag_recv.at[i],
            device_id=(i * step, tp), device_id_type=MESH,
        )

    @pl.when(owner)
    def _():
        def gather(d, total):
            source, arrival = rs_arrival(d)
            arrival.wait_recv()
            return total + rsb[source]

        red[mine] = lax.fori_loop(1, n_ctx, gather, part[mine])

        @pl.loop(1, n_ctx)
        def _(d):
            ag_copy(d).start()

    @pl.loop(0, tiles)
    def _(i):
        cols = pl.ds(pl.multiple_of(i * LANES, LANES), LANES)

        @pl.when(me < n_ctx - 1)
        def _():
            g_copy(i).wait_recv()
            mg[:, cols] += jnp.dot(a2[i], by_group(gn[i]), preferred_element_type=jnp.float32)

        z = mg[:, cols]
        kg_ref[:, cols] = (z * v_ref[:, cols].astype(jnp.float32)).astype(jnp.bfloat16)
        vg_ref[:, cols] = (z * k_ref[:, cols].astype(jnp.float32)).astype(jnp.bfloat16)

    for i in range(tiles):
        @pl.when(i * step != me)
        def _():
            ag_arrival(i).wait_recv()

        fg_ref[pl.ds(i * per_tile, per_tile), :] = red[i, pl.ds(0, per_tile), :]
        sg_ref[:, pl.ds(i * LANES, LANES)] = jnp.sum(red[i, pl.ds(per_tile, 8), :], axis=0, keepdims=True)

    for p in range(PIECES):
        for n, peer in enumerate(direct):
            og_copy(p, n, peer).wait_send()
        for n, a in enumerate(across):
            forward_copy(a, p, n).wait_send()

    @pl.when(me < n_ctx - 1)
    def _():
        x_copy.wait_send()

    @pl.when(me > 0)
    def _():
        @pl.loop(0, tiles)
        def _(i):
            g_copy(i).wait_send()

    @pl.loop(0, tiles)
    def _(i):
        @pl.when(i * step != me)
        def _():
            rs_copy(i).wait_send()

    @pl.when(owner)
    def _():
        @pl.loop(1, n_ctx)
        def _(d):
            ag_copy(d).wait_send()


def write_out(*refs):
    sem = refs[10]
    copies = [pltpu.make_async_copy(refs[n], refs[5 + n], sem.at[n]) for n in range(5)]
    for copy in copies:
        copy.start()
    for copy in copies:
        copy.wait()


def on_device(n_ctx, n_tp, q, k, v, filters, skip_gain, out_grad, w_out):
    rows, channels = q.shape
    tiles = channels // LANES
    groups = filters.shape[0]
    block = (groups // tiles) + 8
    anywhere = pl.BlockSpec(memory_space=pl.ANY)
    vmem = pl.BlockSpec(memory_space=pltpu.VMEM)
    bf, fl = jnp.bfloat16, jnp.float32
    dma = pltpu.SemaphoreType.DMA
    table = pltpu.VMEM((tiles, rows, (groups // tiles) * LANES), bf)
    slab = pltpu.VMEM((tiles, rows, LANES), bf)
    out = pl.pallas_call(
        functools.partial(kernel, n_ctx, n_tp),
        out_shape=(
            jax.ShapeDtypeStruct((rows, channels), bf),
            jax.ShapeDtypeStruct((rows, channels), bf),
            jax.ShapeDtypeStruct((rows, channels), bf),
            jax.ShapeDtypeStruct(filters.shape, fl),
            jax.ShapeDtypeStruct((1, channels), fl),
        ),
        in_specs=[anywhere] * 7,
        out_specs=(vmem,) * 5,
        scratch_shapes=[
            pltpu.VMEM((rows, channels), bf),
            pltpu.VMEM((rows, channels), bf),
            pltpu.VMEM((rows, channels), bf),
            pltpu.VMEM(filters.shape, fl),
            pltpu.VMEM((1, channels), fl),
            pltpu.VMEM((rows, channels), bf),
            dma((6,)),
            pltpu.VMEM((n_tp, channels, channels), bf),
            pltpu.VMEM((n_tp, PIECES, rows, channels // PIECES), bf),
            slab, slab, slab, slab,
            table, table, table, table,
            pltpu.VMEM((rows, channels), fl),
            pltpu.VMEM((rows, channels), fl),
            pltpu.VMEM((tiles, block, LANES), fl),
            pltpu.VMEM((n_ctx, block, LANES), fl),
            pltpu.VMEM((tiles, block, LANES), fl),
            dma((n_tp,)),
            dma((n_tp // 2, PIECES)),
            dma((n_tp, PIECES)),
            dma((n_tp // 2, PIECES)),
            dma, dma,
            dma((tiles,)), dma((tiles,)),
            dma((tiles,)), dma((n_ctx,)),
            dma((n_ctx,)), dma((tiles,)),
        ],
        compiler_params=pltpu.CompilerParams(
            collective_id=0, has_side_effects=True, vmem_limit_bytes=56 * 1024 * 1024
        ),
        cost_estimate=pl.CostEstimate(
            flops=2 * rows * channels * channels * n_tp, bytes_accessed=2 * channels * channels * n_tp, transcendentals=0
        ),
    )(q, k, v, filters, skip_gain.reshape(1, channels), out_grad, w_out)
    out = pl.pallas_call(
        write_out,
        out_shape=[jax.ShapeDtypeStruct(o.shape, o.dtype) for o in out],
        in_specs=[anywhere] * 5,
        out_specs=[anywhere] * 5,
        scratch_shapes=[dma((5,))],
    )(*out)
    return (out[0], out[1], out[2], out[3], out[4].reshape(channels))


def solution(mesh):
    n_ctx, n_tp = mesh.shape["ctx"], mesh.shape["tp"]
    return jax.shard_map(
        functools.partial(on_device, n_ctx, n_tp),
        mesh=mesh,
        in_specs=(
            P("ctx", "tp"),
            P("ctx", "tp"),
            P("ctx", "tp"),
            P("tp", None),
            P("tp"),
            P("ctx", "tp"),
            P("tp", None),
        ),
        out_specs=(P("ctx", "tp"), P("ctx", "tp"), P("ctx", "tp"), P("tp", None), P("tp")),
        check_vma=False,
    )
```

```python
import functools

import jax
import jax.numpy as jnp
from jax import lax
from jax.experimental import pallas as pl
from jax.experimental.pallas import tpu as pltpu
from jax.sharding import PartitionSpec as P

MESH = pl.DeviceIdType.MESH
LANES = 128
NT = (((1,), (1,)), ((), ()))
PIECES = 2


def kernel(
    n_ctx, n_tp,
    q_hbm, k_hbm, v_hbm, f_hbm, s_hbm, og_hbm, w_hbm,
    qg_ref, kg_ref, vg_ref, fg_ref, sg_ref,
    q_ref, k_ref, v_ref, f_ref, s_ref, og_ref, in_sem,
    wv, ogb, x, xp, g, gn, a1, b1, a2, b2, mg, filt, part, rsb, red,
    w_sem, og_send, og_recv, fw_send, x_send, x_recv, g_send, g_recv,
    rs_send, rs_recv, ag_send, ag_recv,
):
    rows, channels = q_ref.shape
    tiles = channels // LANES
    per_tile = f_ref.shape[0] // tiles
    span = LANES // per_tile
    wide = channels // PIECES
    step = n_ctx // tiles
    me = lax.axis_index("ctx")
    tp = lax.axis_index("tp")
    mate = tp + 1 - 2 * lax.rem(tp, 2)
    across = [lax.rem(tp + 2 * d, n_tp) for d in range(1, n_tp // 2)]
    across_mate = [a + 1 - 2 * lax.rem(a, 2) for a in across]
    order = [tp, mate] + across + across_mate

    def bring(n, source, target):
        copy = pltpu.make_async_copy(source, target, in_sem.at[n])
        copy.start()
        return copy

    k_in = bring(0, k_hbm, k_ref)
    v_in = bring(1, v_hbm, v_ref)
    og_in = bring(2, og_hbm, og_ref)
    f_in = bring(3, f_hbm, f_ref)
    s_in = bring(4, s_hbm, s_ref)
    q_in = bring(5, q_hbm, q_ref)

    w_copies = []
    for n, slot in enumerate(order):
        copy = pltpu.make_async_copy(
            w_hbm.at[:, pl.ds(pl.multiple_of(slot * channels, channels), channels)], wv.at[n], w_sem.at[n]
        )
        copy.start()
        w_copies.append(copy)

    barrier = pltpu.get_barrier_semaphore()
    for peer in order[1:]:
        pl.semaphore_signal(barrier, inc=1, device_id=(me, peer), device_id_type=MESH)

    @pl.loop(1, n_ctx)
    def _(d):
        pl.semaphore_signal(barrier, inc=1, device_id=(lax.rem(me + d, n_ctx), tp), device_id_type=MESH)

    k_in.wait()
    v_in.wait()

    @pl.loop(0, tiles)
    def _(i):
        cols = pl.ds(pl.multiple_of(i * LANES, LANES), LANES)
        x[i] = (k_ref[:, cols].astype(jnp.float32) * v_ref[:, cols].astype(jnp.float32)).astype(jnp.bfloat16)

    og_in.wait()
    pl.semaphore_wait(barrier, n_tp - 1 + n_ctx - 1)

    def og_copy(p, n, peer):
        return pltpu.make_async_remote_copy(
            src_ref=og_ref.at[:, pl.ds(p * wide, wide)], dst_ref=ogb.at[tp, p],
            send_sem=og_send.at[n, p], recv_sem=og_recv.at[tp, p],
            device_id=(me, peer), device_id_type=MESH,
        )

    def forward_copy(slot, p, n):
        return pltpu.make_async_remote_copy(
            src_ref=ogb.at[slot, p], dst_ref=ogb.at[slot, p],
            send_sem=fw_send.at[n, p], recv_sem=og_recv.at[slot, p],
            device_id=(me, mate), device_id_type=MESH,
        )

    direct = across + [mate]
    for p in range(PIECES):
        for n, peer in enumerate(direct):
            og_copy(p, n, peer).start()

    x_copy = pltpu.make_async_remote_copy(
        src_ref=x, dst_ref=xp, send_sem=x_send, recv_sem=x_recv,
        device_id=(lax.rem(me + 1, n_ctx), tp), device_id_type=MESH,
    )

    @pl.when(me < n_ctx - 1)
    def _():
        x_copy.start()

    f_in.wait()
    row = lax.broadcasted_iota(jnp.int32, (rows, LANES), 0)
    col = lax.broadcasted_iota(jnp.int32, (rows, LANES), 1)
    mirror = jnp.where(lax.rem(row + col, LANES) == 0, 1.0, 0.0).astype(jnp.bfloat16)

    def spread(line):
        return pltpu.roll(jnp.broadcast_to(line, (rows, LANES)), 0, 1, stride=1, stride_axis=0)

    @pl.loop(0, tiles)
    def _(i):
        taps = f_ref[pl.ds(pl.multiple_of(i * per_tile, per_tile), per_tile), :]
        back = jnp.dot(taps.astype(jnp.bfloat16), mirror, preferred_element_type=jnp.float32)
        for j in range(per_tile):
            at = pl.ds(j * LANES, LANES)
            c1 = spread(back[j : j + 1])
            a1[i, :, at] = jnp.where(col > row, c1, 0.0).astype(jnp.bfloat16)
            b1[i, :, at] = jnp.where(col <= row, c1, 0.0).astype(jnp.bfloat16)
            c2 = spread(taps[j : j + 1])
            a2[i, :, at] = jnp.where(col < row, c2, 0.0).astype(jnp.bfloat16)
            b2[i, :, at] = jnp.where(col >= row, c2, 0.0).astype(jnp.bfloat16)

    lane = lax.broadcasted_iota(jnp.int32, (1, LANES), 1)
    masks = [
        jnp.where((lane >= j * span) & (lane < (j + 1) * span), 1.0, 0.0).astype(jnp.bfloat16)
        for j in range(per_tile)
    ]

    def by_group(block):
        return jnp.concatenate([block * m for m in masks], axis=0)

    def project(n, block_of, first):
        @pl.loop(0, tiles // 2)
        def _(i):
            chans = pl.ds(pl.multiple_of(i * 2 * LANES, 2 * LANES), 2 * LANES)
            total = None
            for p in range(PIECES):
                term = lax.dot_general(
                    block_of(p), wv[n, chans, pl.ds(p * wide, wide)], NT, preferred_element_type=jnp.float32
                )
                total = term if total is None else total + term
            if first:
                mg[:, chans] = total
            else:
                mg[:, chans] += total

    w_copies[0].wait()
    project(0, lambda p: og_ref[:, pl.ds(p * wide, wide)], True)

    for p in range(PIECES):
        forward_copy(mate, p, 0).wait_recv()
    w_copies[1].wait()
    project(1, lambda p: ogb[mate, p], False)

    @pl.when(me > 0)
    def _():
        x_copy.wait_recv()

    @pl.when(me == 0)
    def _():
        xp[...] = jnp.zeros_like(xp)

    for p in range(PIECES):
        for n, a in enumerate(across):
            forward_copy(a, p, n).wait_recv()
            forward_copy(a, p, n).start()

    s_in.wait()

    @pl.loop(0, tiles)
    def _(i):
        cols = pl.ds(pl.multiple_of(i * LANES, LANES), LANES)
        y = jnp.dot(a1[i], by_group(xp[i]), preferred_element_type=jnp.float32)
        y += jnp.dot(b1[i], by_group(x[i]), preferred_element_type=jnp.float32)
        filt[:, cols] = y + s_ref[:, cols] * x[i].astype(jnp.float32)

    for n, a in enumerate(across):
        w_copies[2 + n].wait()
        project(2 + n, lambda p, a=a: ogb[a, p], False)
    for n, a in enumerate(across_mate):
        for p in range(PIECES):
            forward_copy(a, p, n).wait_recv()
        w_copies[2 + len(across) + n].wait()
        project(2 + len(across) + n, lambda p, a=a: ogb[a, p], False)

    q_in.wait()

    def g_copy(i):
        return pltpu.make_async_remote_copy(
            src_ref=g.at[i], dst_ref=gn.at[i], send_sem=g_send.at[i], recv_sem=g_recv.at[i],
            device_id=(lax.rem(me + n_ctx - 1, n_ctx), tp), device_id_type=MESH,
        )

    @pl.loop(0, tiles)
    def _(i):
        cols = pl.ds(pl.multiple_of(i * LANES, LANES), LANES)
        m = mg[:, cols]
        g[i] = (m * q_ref[:, cols].astype(jnp.float32)).astype(jnp.bfloat16)

        @pl.when(me > 0)
        def _():
            g_copy(i).start()

        qg_ref[:, cols] = (m * filt[:, cols]).astype(jnp.bfloat16)

    flip = jnp.where(row + col == rows - 1, 1.0, 0.0).astype(jnp.bfloat16)

    def upside_down(block):
        return jnp.dot(flip, block, preferred_element_type=jnp.float32).astype(jnp.bfloat16)

    @pl.loop(0, tiles)
    def _(i):
        gt = g[i]
        far = lax.dot_general(by_group(upside_down(xp[i])), gt, NT, preferred_element_type=jnp.float32)
        near = lax.dot_general(by_group(upside_down(x[i])), gt, NT, preferred_element_type=jnp.float32)
        for j in range(per_tile):
            at = slice(j * rows, (j + 1) * rows)
            pairs = jnp.where(col + row >= rows - 1, near[at], far[at])
            turned = pltpu.roll(pairs, 0, 1, stride=1, stride_axis=0)
            part[i, pl.ds(j, 1), :] = jnp.sum(turned, axis=0, keepdims=True)
        part[i, pl.ds(0, per_tile), :] = pltpu.roll(part[i, pl.ds(0, per_tile), :], 1, 1)
        both = gt.astype(jnp.float32) * x[i].astype(jnp.float32)
        part[i, pl.ds(per_tile, 8), :] = jnp.sum(both.reshape(rows // 8, 8, LANES), axis=0)

    def rs_copy(i):
        return pltpu.make_async_remote_copy(
            src_ref=part.at[i], dst_ref=rsb.at[me], send_sem=rs_send.at[i], recv_sem=rs_recv.at[me],
            device_id=(i * step, tp), device_id_type=MESH,
        )

    def rs_arrival(d):
        source = lax.rem(me + d, n_ctx)
        return source, pltpu.make_async_remote_copy(
            src_ref=part.at[0], dst_ref=rsb.at[source], send_sem=rs_send.at[0], recv_sem=rs_recv.at[source],
            device_id=(source, tp), device_id_type=MESH,
        )

    mine = me // step
    owner = lax.rem(me, step) == 0

    @pl.loop(0, tiles)
    def _(i):
        @pl.when(i * step != me)
        def _():
            rs_copy(i).start()

    @pl.loop(0, tiles)
    def _(i):
        cols = pl.ds(pl.multiple_of(i * LANES, LANES), LANES)
        z = jnp.dot(b2[i], by_group(g[i]), preferred_element_type=jnp.float32)
        mg[:, cols] = z + s_ref[:, cols] * g[i].astype(jnp.float32)

    def ag_copy(d):
        return pltpu.make_async_remote_copy(
            src_ref=red.at[mine], dst_ref=red.at[mine], send_sem=ag_send.at[d], recv_sem=ag_recv.at[mine],
            device_id=(lax.rem(me + d, n_ctx), tp), device_id_type=MESH,
        )

    def ag_arrival(i):
        return pltpu.make_async_remote_copy(
            src_ref=red.at[i], dst_ref=red.at[i], send_sem=ag_send.at[0], recv_sem=ag_recv.at[i],
            device_id=(i * step, tp), device_id_type=MESH,
        )

    @pl.when(owner)
    def _():
        def gather(d, total):
            source, arrival = rs_arrival(d)
            arrival.wait_recv()
            return total + rsb[source]

        red[mine] = lax.fori_loop(1, n_ctx, gather, part[mine])

        @pl.loop(1, n_ctx)
        def _(d):
            ag_copy(d).start()

    @pl.loop(0, tiles)
    def _(i):
        cols = pl.ds(pl.multiple_of(i * LANES, LANES), LANES)

        @pl.when(me < n_ctx - 1)
        def _():
            g_copy(i).wait_recv()
            mg[:, cols] += jnp.dot(a2[i], by_group(gn[i]), preferred_element_type=jnp.float32)

        z = mg[:, cols]
        kg_ref[:, cols] = (z * v_ref[:, cols].astype(jnp.float32)).astype(jnp.bfloat16)
        vg_ref[:, cols] = (z * k_ref[:, cols].astype(jnp.float32)).astype(jnp.bfloat16)

    for i in range(tiles):
        @pl.when(i * step != me)
        def _():
            ag_arrival(i).wait_recv()

        fg_ref[pl.ds(i * per_tile, per_tile), :] = red[i, pl.ds(0, per_tile), :]
        sg_ref[:, pl.ds(i * LANES, LANES)] = jnp.sum(red[i, pl.ds(per_tile, 8), :], axis=0, keepdims=True)

    for p in range(PIECES):
        for n, peer in enumerate(direct):
            og_copy(p, n, peer).wait_send()
        for n, a in enumerate(across):
            forward_copy(a, p, n).wait_send()

    @pl.when(me < n_ctx - 1)
    def _():
        x_copy.wait_send()

    @pl.when(me > 0)
    def _():
        @pl.loop(0, tiles)
        def _(i):
            g_copy(i).wait_send()

    @pl.loop(0, tiles)
    def _(i):
        @pl.when(i * step != me)
        def _():
            rs_copy(i).wait_send()

    @pl.when(owner)
    def _():
        @pl.loop(1, n_ctx)
        def _(d):
            ag_copy(d).wait_send()


def write_out(*refs):
    held, sem = refs[10:15], refs[15]
    ins = [pltpu.make_async_copy(refs[n], held[n], sem.at[0, n]) for n in range(5)]
    outs = [pltpu.make_async_copy(held[n], refs[5 + n], sem.at[1, n]) for n in range(5)]
    for copy in ins:
        copy.start()
    for n in range(5):
        ins[n].wait()
        outs[n].start()
    for copy in outs:
        copy.wait()


def on_device(n_ctx, n_tp, q, k, v, filters, skip_gain, out_grad, w_out):
    rows, channels = q.shape
    tiles = channels // LANES
    groups = filters.shape[0]
    block = (groups // tiles) + 8
    vmem = pl.BlockSpec(memory_space=pltpu.VMEM)
    bf, fl = jnp.bfloat16, jnp.float32
    dma = pltpu.SemaphoreType.DMA
    table = pltpu.VMEM((tiles, rows, (groups // tiles) * LANES), bf)
    slab = pltpu.VMEM((tiles, rows, LANES), bf)
    out = pl.pallas_call(
        functools.partial(kernel, n_ctx, n_tp),
        out_shape=(
            jax.ShapeDtypeStruct((rows, channels), bf),
            jax.ShapeDtypeStruct((rows, channels), bf),
            jax.ShapeDtypeStruct((rows, channels), bf),
            jax.ShapeDtypeStruct(filters.shape, fl),
            jax.ShapeDtypeStruct((1, channels), fl),
        ),
        in_specs=[pl.BlockSpec(memory_space=pltpu.HBM)] * 7,
        out_specs=(vmem,) * 5,
        scratch_shapes=[
            pltpu.VMEM((rows, channels), bf),
            pltpu.VMEM((rows, channels), bf),
            pltpu.VMEM((rows, channels), bf),
            pltpu.VMEM(filters.shape, fl),
            pltpu.VMEM((1, channels), fl),
            pltpu.VMEM((rows, channels), bf),
            dma((6,)),
            pltpu.VMEM((n_tp, channels, channels), bf),
            pltpu.VMEM((n_tp, PIECES, rows, channels // PIECES), bf),
            slab, slab, slab, slab,
            table, table, table, table,
            pltpu.VMEM((rows, channels), fl),
            pltpu.VMEM((rows, channels), fl),
            pltpu.VMEM((tiles, block, LANES), fl),
            pltpu.VMEM((n_ctx, block, LANES), fl),
            pltpu.VMEM((tiles, block, LANES), fl),
            dma((n_tp,)),
            dma((n_tp // 2, PIECES)),
            dma((n_tp, PIECES)),
            dma((n_tp // 2, PIECES)),
            dma, dma,
            dma((tiles,)), dma((tiles,)),
            dma((tiles,)), dma((n_ctx,)),
            dma((n_ctx,)), dma((tiles,)),
        ],
        compiler_params=pltpu.CompilerParams(
            collective_id=0, has_side_effects=True, vmem_limit_bytes=56 * 1024 * 1024
        ),
        cost_estimate=pl.CostEstimate(
            flops=2 * rows * channels * channels * n_tp, bytes_accessed=2 * channels * channels * n_tp, transcendentals=0
        ),
    )(q, k, v, filters, skip_gain.reshape(1, channels), out_grad, w_out)
    out = pl.pallas_call(
        write_out,
        out_shape=[jax.ShapeDtypeStruct(o.shape, o.dtype) for o in out],
        in_specs=[pl.BlockSpec(memory_space=pltpu.HBM)] * 5,
        out_specs=[pl.BlockSpec(memory_space=pltpu.HBM)] * 5,
        scratch_shapes=[pltpu.VMEM(o.shape, o.dtype) for o in out] + [dma((2, 5))],
        compiler_params=pltpu.CompilerParams(vmem_limit_bytes=56 * 1024 * 1024),
    )(*out)
    return (out[0], out[1], out[2], out[3], out[4].reshape(channels))


def solution(mesh):
    n_ctx, n_tp = mesh.shape["ctx"], mesh.shape["tp"]
    return jax.shard_map(
        functools.partial(on_device, n_ctx, n_tp),
        mesh=mesh,
        in_specs=(
            P("ctx", "tp"),
            P("ctx", "tp"),
            P("ctx", "tp"),
            P("tp", None),
            P("tp"),
            P("ctx", "tp"),
            P("tp", None),
        ),
        out_specs=(P("ctx", "tp"), P("ctx", "tp"), P("ctx", "tp"), P("tp", None), P("tp")),
        check_vma=False,
    )
```

```python
import functools

import jax
import jax.numpy as jnp
from jax import lax
from jax.experimental import pallas as pl
from jax.experimental.pallas import tpu as pltpu
from jax.sharding import PartitionSpec as P

MESH = pl.DeviceIdType.MESH
LANES = 128
NT = (((1,), (1,)), ((), ()))
PIECES = 2


def kernel(
    n_ctx, n_tp,
    q_hbm, k_hbm, v_hbm, f_hbm, s_hbm, og_hbm, w_hbm,
    qg_ref, kg_ref, vg_ref, fg_ref, sg_ref,
    q_ref, k_ref, v_ref, f_ref, s_ref, og_ref, in_sem,
    wv, ogb, x, xp, g, gn, a1, b1, a2, b2, mg, part, rsb, red,
    w_sem, og_send, og_recv, fw_send, x_send, x_recv, g_send, g_recv,
    rs_send, rs_recv, ag_send, ag_recv,
):
    rows, channels = q_ref.shape
    tiles = channels // LANES
    per_tile = f_ref.shape[0] // tiles
    span = LANES // per_tile
    wide = channels // PIECES
    step = n_ctx // tiles
    me = lax.axis_index("ctx")
    tp = lax.axis_index("tp")
    mate = tp + 1 - 2 * lax.rem(tp, 2)
    across = [lax.rem(tp + 2 * d, n_tp) for d in range(1, n_tp // 2)]
    across_mate = [a + 1 - 2 * lax.rem(a, 2) for a in across]
    order = [tp, mate] + across + across_mate

    def bring(n, source, target):
        copy = pltpu.make_async_copy(source, target, in_sem.at[n])
        copy.start()
        return copy

    k_in = bring(0, k_hbm, k_ref)
    v_in = bring(1, v_hbm, v_ref)
    og_in = bring(2, og_hbm, og_ref)
    f_in = bring(3, f_hbm, f_ref)
    s_in = bring(4, s_hbm, s_ref)
    q_in = bring(5, q_hbm, q_ref)

    w_copies = []
    for n, slot in enumerate(order):
        copy = pltpu.make_async_copy(
            w_hbm.at[:, pl.ds(pl.multiple_of(slot * channels, channels), channels)], wv.at[n], w_sem.at[n]
        )
        copy.start()
        w_copies.append(copy)

    barrier = pltpu.get_barrier_semaphore()
    for peer in order[1:]:
        pl.semaphore_signal(barrier, inc=1, device_id=(me, peer), device_id_type=MESH)

    @pl.loop(1, n_ctx)
    def _(d):
        pl.semaphore_signal(barrier, inc=1, device_id=(lax.rem(me + d, n_ctx), tp), device_id_type=MESH)

    k_in.wait()
    v_in.wait()

    @pl.loop(0, tiles)
    def _(i):
        cols = pl.ds(pl.multiple_of(i * LANES, LANES), LANES)
        x[i] = (k_ref[:, cols].astype(jnp.float32) * v_ref[:, cols].astype(jnp.float32)).astype(jnp.bfloat16)

    og_in.wait()
    pl.semaphore_wait(barrier, n_tp - 1 + n_ctx - 1)

    def og_copy(p, n, peer):
        return pltpu.make_async_remote_copy(
            src_ref=og_ref.at[:, pl.ds(p * wide, wide)], dst_ref=ogb.at[tp, p],
            send_sem=og_send.at[n, p], recv_sem=og_recv.at[tp, p],
            device_id=(me, peer), device_id_type=MESH,
        )

    def forward_copy(slot, p, n):
        return pltpu.make_async_remote_copy(
            src_ref=ogb.at[slot, p], dst_ref=ogb.at[slot, p],
            send_sem=fw_send.at[n, p], recv_sem=og_recv.at[slot, p],
            device_id=(me, mate), device_id_type=MESH,
        )

    direct = across + [mate]
    for p in range(PIECES):
        for n, peer in enumerate(direct):
            og_copy(p, n, peer).start()

    x_copy = pltpu.make_async_remote_copy(
        src_ref=x, dst_ref=xp, send_sem=x_send, recv_sem=x_recv,
        device_id=(lax.rem(me + 1, n_ctx), tp), device_id_type=MESH,
    )

    @pl.when(me < n_ctx - 1)
    def _():
        x_copy.start()

    f_in.wait()
    row = lax.broadcasted_iota(jnp.int32, (rows, LANES), 0)
    col = lax.broadcasted_iota(jnp.int32, (rows, LANES), 1)
    mirror = jnp.where(lax.rem(row + col, LANES) == 0, 1.0, 0.0).astype(jnp.bfloat16)

    def spread(line):
        return pltpu.roll(jnp.broadcast_to(line, (rows, LANES)), 0, 1, stride=1, stride_axis=0)

    @pl.loop(0, tiles, unroll=4)
    def _(i):
        taps = f_ref[pl.ds(pl.multiple_of(i * per_tile, per_tile), per_tile), :]
        back = jnp.dot(taps.astype(jnp.bfloat16), mirror, preferred_element_type=jnp.float32)
        for j in range(per_tile):
            at = pl.ds(j * LANES, LANES)
            c1 = spread(back[j : j + 1])
            a1[i, :, at] = jnp.where(col > row, c1, 0.0).astype(jnp.bfloat16)
            b1[i, :, at] = jnp.where(col <= row, c1, 0.0).astype(jnp.bfloat16)
            c2 = spread(taps[j : j + 1])
            a2[i, :, at] = jnp.where(col < row, c2, 0.0).astype(jnp.bfloat16)
            b2[i, :, at] = jnp.where(col >= row, c2, 0.0).astype(jnp.bfloat16)

    lane = lax.broadcasted_iota(jnp.int32, (1, LANES), 1)
    masks = [
        jnp.where((lane >= j * span) & (lane < (j + 1) * span), 1.0, 0.0).astype(jnp.bfloat16)
        for j in range(per_tile)
    ]

    def by_group(block):
        return jnp.concatenate([block * m for m in masks], axis=0)

    def project(n, block_of, first):
        @pl.loop(0, tiles // 2, unroll=4)
        def _(i):
            chans = pl.ds(pl.multiple_of(i * 2 * LANES, 2 * LANES), 2 * LANES)
            total = None
            for p in range(PIECES):
                term = lax.dot_general(
                    block_of(p), wv[n, chans, pl.ds(p * wide, wide)], NT, preferred_element_type=jnp.float32
                )
                total = term if total is None else total + term
            if first:
                mg[:, chans] = total
            else:
                mg[:, chans] += total

    w_copies[0].wait()
    project(0, lambda p: og_ref[:, pl.ds(p * wide, wide)], True)

    for p in range(PIECES):
        forward_copy(mate, p, 0).wait_recv()
    w_copies[1].wait()
    project(1, lambda p: ogb[mate, p], False)

    @pl.when(me > 0)
    def _():
        x_copy.wait_recv()

    @pl.when(me == 0)
    def _():
        xp[...] = jnp.zeros_like(xp)

    for p in range(PIECES):
        for n, a in enumerate(across):
            forward_copy(a, p, n).wait_recv()
            forward_copy(a, p, n).start()

    for n, a in enumerate(across):
        w_copies[2 + n].wait()
        project(2 + n, lambda p, a=a: ogb[a, p], False)
    for n, a in enumerate(across_mate):
        for p in range(PIECES):
            forward_copy(a, p, n).wait_recv()
        w_copies[2 + len(across) + n].wait()
        project(2 + len(across) + n, lambda p, a=a: ogb[a, p], False)

    q_in.wait()

    def g_copy(i):
        return pltpu.make_async_remote_copy(
            src_ref=g.at[i], dst_ref=gn.at[i], send_sem=g_send.at[i], recv_sem=g_recv.at[i],
            device_id=(lax.rem(me + n_ctx - 1, n_ctx), tp), device_id_type=MESH,
        )

    @pl.loop(0, tiles)
    def _(i):
        cols = pl.ds(pl.multiple_of(i * LANES, LANES), LANES)
        m = mg[:, cols]
        g[i] = (m * q_ref[:, cols].astype(jnp.float32)).astype(jnp.bfloat16)

        @pl.when(me > 0)
        def _():
            g_copy(i).start()

    flip = jnp.where(row + col == rows - 1, 1.0, 0.0).astype(jnp.bfloat16)

    def upside_down(block):
        return jnp.dot(flip, block, preferred_element_type=jnp.float32).astype(jnp.bfloat16)

    @pl.loop(0, tiles, unroll=4)
    def _(i):
        gt = g[i]
        far = lax.dot_general(by_group(upside_down(xp[i])), gt, NT, preferred_element_type=jnp.float32)
        near = lax.dot_general(by_group(upside_down(x[i])), gt, NT, preferred_element_type=jnp.float32)
        for j in range(per_tile):
            at = slice(j * rows, (j + 1) * rows)
            pairs = jnp.where(col + row >= rows - 1, near[at], far[at])
            turned = pltpu.roll(pairs, 0, 1, stride=1, stride_axis=0)
            part[i, pl.ds(j, 1), :] = jnp.sum(turned, axis=0, keepdims=True)
        part[i, pl.ds(0, per_tile), :] = pltpu.roll(part[i, pl.ds(0, per_tile), :], 1, 1)
        both = gt.astype(jnp.float32) * x[i].astype(jnp.float32)
        part[i, pl.ds(per_tile, 8), :] = jnp.sum(both.reshape(rows // 8, 8, LANES), axis=0)

    def rs_copy(i):
        return pltpu.make_async_remote_copy(
            src_ref=part.at[i], dst_ref=rsb.at[me], send_sem=rs_send.at[i], recv_sem=rs_recv.at[me],
            device_id=(i * step, tp), device_id_type=MESH,
        )

    def rs_arrival(d):
        source = lax.rem(me + d, n_ctx)
        return source, pltpu.make_async_remote_copy(
            src_ref=part.at[0], dst_ref=rsb.at[source], send_sem=rs_send.at[0], recv_sem=rs_recv.at[source],
            device_id=(source, tp), device_id_type=MESH,
        )

    mine = me // step
    owner = lax.rem(me, step) == 0

    @pl.loop(0, tiles)
    def _(i):
        @pl.when(i * step != me)
        def _():
            rs_copy(i).start()

    s_in.wait()

    @pl.loop(0, tiles, unroll=4)
    def _(i):
        cols = pl.ds(pl.multiple_of(i * LANES, LANES), LANES)
        y = jnp.dot(a1[i], by_group(xp[i]), preferred_element_type=jnp.float32)
        y += jnp.dot(b1[i], by_group(x[i]), preferred_element_type=jnp.float32)
        y += s_ref[:, cols] * x[i].astype(jnp.float32)
        qg_ref[:, cols] = (mg[:, cols] * y).astype(jnp.bfloat16)

    @pl.loop(0, tiles, unroll=4)
    def _(i):
        cols = pl.ds(pl.multiple_of(i * LANES, LANES), LANES)
        z = jnp.dot(b2[i], by_group(g[i]), preferred_element_type=jnp.float32)
        mg[:, cols] = z + s_ref[:, cols] * g[i].astype(jnp.float32)

    def ag_copy(d):
        return pltpu.make_async_remote_copy(
            src_ref=red.at[mine], dst_ref=red.at[mine], send_sem=ag_send.at[d], recv_sem=ag_recv.at[mine],
            device_id=(lax.rem(me + d, n_ctx), tp), device_id_type=MESH,
        )

    def ag_arrival(i):
        return pltpu.make_async_remote_copy(
            src_ref=red.at[i], dst_ref=red.at[i], send_sem=ag_send.at[0], recv_sem=ag_recv.at[i],
            device_id=(i * step, tp), device_id_type=MESH,
        )

    @pl.when(owner)
    def _():
        def gather(d, total):
            source, arrival = rs_arrival(d)
            arrival.wait_recv()
            return total + rsb[source]

        red[mine] = lax.fori_loop(1, n_ctx, gather, part[mine])

        @pl.loop(1, n_ctx)
        def _(d):
            ag_copy(d).start()

    @pl.loop(0, tiles)
    def _(i):
        cols = pl.ds(pl.multiple_of(i * LANES, LANES), LANES)

        @pl.when(me < n_ctx - 1)
        def _():
            g_copy(i).wait_recv()
            mg[:, cols] += jnp.dot(a2[i], by_group(gn[i]), preferred_element_type=jnp.float32)

        z = mg[:, cols]
        kg_ref[:, cols] = (z * v_ref[:, cols].astype(jnp.float32)).astype(jnp.bfloat16)
        vg_ref[:, cols] = (z * k_ref[:, cols].astype(jnp.float32)).astype(jnp.bfloat16)

    for i in range(tiles):
        @pl.when(i * step != me)
        def _():
            ag_arrival(i).wait_recv()

        fg_ref[pl.ds(i * per_tile, per_tile), :] = red[i, pl.ds(0, per_tile), :]
        sg_ref[:, pl.ds(i * LANES, LANES)] = jnp.sum(red[i, pl.ds(per_tile, 8), :], axis=0, keepdims=True)

    for p in range(PIECES):
        for n, peer in enumerate(direct):
            og_copy(p, n, peer).wait_send()
        for n, a in enumerate(across):
            forward_copy(a, p, n).wait_send()

    @pl.when(me < n_ctx - 1)
    def _():
        x_copy.wait_send()

    @pl.when(me > 0)
    def _():
        @pl.loop(0, tiles)
        def _(i):
            g_copy(i).wait_send()

    @pl.loop(0, tiles)
    def _(i):
        @pl.when(i * step != me)
        def _():
            rs_copy(i).wait_send()

    @pl.when(owner)
    def _():
        @pl.loop(1, n_ctx)
        def _(d):
            ag_copy(d).wait_send()


def write_out(*refs):
    held, sem = refs[10:15], refs[15]
    ins = [pltpu.make_async_copy(refs[n], held[n], sem.at[0, n]) for n in range(5)]
    outs = [pltpu.make_async_copy(held[n], refs[5 + n], sem.at[1, n]) for n in range(5)]
    for copy in ins:
        copy.start()
    for n in range(5):
        ins[n].wait()
        outs[n].start()
    for copy in outs:
        copy.wait()


def on_device(n_ctx, n_tp, q, k, v, filters, skip_gain, out_grad, w_out):
    rows, channels = q.shape
    tiles = channels // LANES
    groups = filters.shape[0]
    block = (groups // tiles) + 8
    vmem = pl.BlockSpec(memory_space=pltpu.VMEM)
    bf, fl = jnp.bfloat16, jnp.float32
    dma = pltpu.SemaphoreType.DMA
    table = pltpu.VMEM((tiles, rows, (groups // tiles) * LANES), bf)
    slab = pltpu.VMEM((tiles, rows, LANES), bf)
    out = pl.pallas_call(
        functools.partial(kernel, n_ctx, n_tp),
        out_shape=(
            jax.ShapeDtypeStruct((rows, channels), bf),
            jax.ShapeDtypeStruct((rows, channels), bf),
            jax.ShapeDtypeStruct((rows, channels), bf),
            jax.ShapeDtypeStruct(filters.shape, fl),
            jax.ShapeDtypeStruct((1, channels), fl),
        ),
        in_specs=[pl.BlockSpec(memory_space=pltpu.HBM)] * 7,
        out_specs=(vmem,) * 5,
        scratch_shapes=[
            pltpu.VMEM((rows, channels), bf),
            pltpu.VMEM((rows, channels), bf),
            pltpu.VMEM((rows, channels), bf),
            pltpu.VMEM(filters.shape, fl),
            pltpu.VMEM((1, channels), fl),
            pltpu.VMEM((rows, channels), bf),
            dma((6,)),
            pltpu.VMEM((n_tp, channels, channels), bf),
            pltpu.VMEM((n_tp, PIECES, rows, channels // PIECES), bf),
            slab, slab, slab, slab,
            table, table, table, table,
            pltpu.VMEM((rows, channels), fl),
            pltpu.VMEM((tiles, block, LANES), fl),
            pltpu.VMEM((n_ctx, block, LANES), fl),
            pltpu.VMEM((tiles, block, LANES), fl),
            dma((n_tp,)),
            dma((n_tp // 2, PIECES)),
            dma((n_tp, PIECES)),
            dma((n_tp // 2, PIECES)),
            dma, dma,
            dma((tiles,)), dma((tiles,)),
            dma((tiles,)), dma((n_ctx,)),
            dma((n_ctx,)), dma((tiles,)),
        ],
        compiler_params=pltpu.CompilerParams(
            collective_id=0, has_side_effects=True, vmem_limit_bytes=56 * 1024 * 1024
        ),
        cost_estimate=pl.CostEstimate(
            flops=2 * rows * channels * channels * n_tp, bytes_accessed=2 * channels * channels * n_tp, transcendentals=0
        ),
    )(q, k, v, filters, skip_gain.reshape(1, channels), out_grad, w_out)
    out = pl.pallas_call(
        write_out,
        out_shape=[jax.ShapeDtypeStruct(o.shape, o.dtype) for o in out],
        in_specs=[pl.BlockSpec(memory_space=pltpu.HBM)] * 5,
        out_specs=[pl.BlockSpec(memory_space=pltpu.HBM)] * 5,
        scratch_shapes=[pltpu.VMEM(o.shape, o.dtype) for o in out] + [dma((2, 5))],
        compiler_params=pltpu.CompilerParams(vmem_limit_bytes=56 * 1024 * 1024),
    )(*out)
    return (out[0], out[1], out[2], out[3], out[4].reshape(channels))


def solution(mesh):
    n_ctx, n_tp = mesh.shape["ctx"], mesh.shape["tp"]
    return jax.shard_map(
        functools.partial(on_device, n_ctx, n_tp),
        mesh=mesh,
        in_specs=(
            P("ctx", "tp"),
            P("ctx", "tp"),
            P("ctx", "tp"),
            P("tp", None),
            P("tp"),
            P("ctx", "tp"),
            P("tp", None),
        ),
        out_specs=(P("ctx", "tp"), P("ctx", "tp"), P("ctx", "tp"), P("tp", None), P("tp")),
        check_vma=False,
    )
```

```python
import functools

import jax
import jax.numpy as jnp
from jax import lax
from jax.experimental import pallas as pl
from jax.experimental.pallas import tpu as pltpu
from jax.sharding import PartitionSpec as P

MESH = pl.DeviceIdType.MESH
LANES = 128
NT = (((1,), (1,)), ((), ()))
PIECES = 2


def kernel(
    n_ctx, n_tp,
    q_hbm, k_hbm, v_hbm, f_hbm, s_hbm, og_hbm, w_hbm,
    qg_ref, kg_ref, vg_ref, fg_ref, sg_ref,
    q_ref, k_ref, v_ref, f_ref, s_ref, og_ref, in_sem,
    wv, ogb, x, xp, g, gn, a1, b1, a2, b2, mg, part, rsb, red,
    w_sem, og_send, og_recv, fw_send, x_send, x_recv, g_send, g_recv,
    rs_send, rs_recv, ag_send, ag_recv,
):
    rows, channels = q_ref.shape
    tiles = channels // LANES
    per_tile = f_ref.shape[0] // tiles
    span = LANES // per_tile
    wide = channels // PIECES
    step = n_ctx // tiles
    me = lax.axis_index("ctx")
    tp = lax.axis_index("tp")
    mate = tp + 1 - 2 * lax.rem(tp, 2)
    across = [lax.rem(tp + 2 * d, n_tp) for d in range(1, n_tp // 2)]
    across_mate = [a + 1 - 2 * lax.rem(a, 2) for a in across]
    order = [tp, mate] + across + across_mate

    def bring(n, source, target):
        copy = pltpu.make_async_copy(source, target, in_sem.at[n])
        copy.start()
        return copy

    k_in = bring(0, k_hbm, k_ref)
    v_in = bring(1, v_hbm, v_ref)
    og_in = bring(2, og_hbm, og_ref)
    f_in = bring(3, f_hbm, f_ref)
    s_in = bring(4, s_hbm, s_ref)
    q_in = bring(5, q_hbm, q_ref)

    w_copies = []
    for n, slot in enumerate(order):
        copy = pltpu.make_async_copy(
            w_hbm.at[:, pl.ds(pl.multiple_of(slot * channels, channels), channels)], wv.at[n], w_sem.at[n]
        )
        copy.start()
        w_copies.append(copy)

    barrier = pltpu.get_barrier_semaphore()
    for peer in order[1:]:
        pl.semaphore_signal(barrier, inc=1, device_id=(me, peer), device_id_type=MESH)

    @pl.loop(1, n_ctx)
    def _(d):
        pl.semaphore_signal(barrier, inc=1, device_id=(lax.rem(me + d, n_ctx), tp), device_id_type=MESH)

    k_in.wait()
    v_in.wait()

    @pl.loop(0, tiles)
    def _(i):
        cols = pl.ds(pl.multiple_of(i * LANES, LANES), LANES)
        x[i] = (k_ref[:, cols].astype(jnp.float32) * v_ref[:, cols].astype(jnp.float32)).astype(jnp.bfloat16)

    og_in.wait()
    pl.semaphore_wait(barrier, n_tp - 1 + n_ctx - 1)

    def og_copy(p, n, peer):
        return pltpu.make_async_remote_copy(
            src_ref=og_ref.at[:, pl.ds(p * wide, wide)], dst_ref=ogb.at[tp, p],
            send_sem=og_send.at[n, p], recv_sem=og_recv.at[tp, p],
            device_id=(me, peer), device_id_type=MESH,
        )

    def forward_copy(slot, p, n):
        return pltpu.make_async_remote_copy(
            src_ref=ogb.at[slot, p], dst_ref=ogb.at[slot, p],
            send_sem=fw_send.at[n, p], recv_sem=og_recv.at[slot, p],
            device_id=(me, mate), device_id_type=MESH,
        )

    direct = across + [mate]
    for p in range(PIECES):
        for n, peer in enumerate(direct):
            og_copy(p, n, peer).start()

    x_copy = pltpu.make_async_remote_copy(
        src_ref=x, dst_ref=xp, send_sem=x_send, recv_sem=x_recv,
        device_id=(lax.rem(me + 1, n_ctx), tp), device_id_type=MESH,
    )

    @pl.when(me < n_ctx - 1)
    def _():
        x_copy.start()

    f_in.wait()
    row = lax.broadcasted_iota(jnp.int32, (rows, LANES), 0)
    col = lax.broadcasted_iota(jnp.int32, (rows, LANES), 1)
    mirror = jnp.where(lax.rem(row + col, LANES) == 0, 1.0, 0.0).astype(jnp.bfloat16)

    above = jnp.where(col > row, 1.0, 0.0).astype(jnp.bfloat16)
    not_above = jnp.where(col <= row, 1.0, 0.0).astype(jnp.bfloat16)
    below = jnp.where(col < row, 1.0, 0.0).astype(jnp.bfloat16)
    not_below = jnp.where(col >= row, 1.0, 0.0).astype(jnp.bfloat16)

    def spread(line):
        return pltpu.roll(jnp.broadcast_to(line, (rows, LANES)), 0, 1, stride=1, stride_axis=0)

    @pl.loop(0, tiles, unroll=4)
    def _(i):
        taps = f_ref[pl.ds(pl.multiple_of(i * per_tile, per_tile), per_tile), :]
        back = jnp.dot(taps.astype(jnp.bfloat16), mirror, preferred_element_type=jnp.float32)
        for j in range(per_tile):
            at = pl.ds(j * LANES, LANES)
            c1 = spread(back[j : j + 1]).astype(jnp.bfloat16)
            a1[i, :, at] = c1 * above
            b1[i, :, at] = c1 * not_above
            c2 = spread(taps[j : j + 1]).astype(jnp.bfloat16)
            a2[i, :, at] = c2 * below
            b2[i, :, at] = c2 * not_below

    lane = lax.broadcasted_iota(jnp.int32, (1, LANES), 1)
    masks = [
        jnp.where((lane >= j * span) & (lane < (j + 1) * span), 1.0, 0.0).astype(jnp.bfloat16)
        for j in range(per_tile)
    ]

    def by_group(block):
        return jnp.concatenate([block * m for m in masks], axis=0)

    def project(n, block_of, first):
        @pl.loop(0, tiles // 2, unroll=4)
        def _(i):
            chans = pl.ds(pl.multiple_of(i * 2 * LANES, 2 * LANES), 2 * LANES)
            total = None
            for p in range(PIECES):
                term = lax.dot_general(
                    block_of(p), wv[n, chans, pl.ds(p * wide, wide)], NT, preferred_element_type=jnp.float32
                )
                total = term if total is None else total + term
            if first:
                mg[:, chans] = total
            else:
                mg[:, chans] += total

    w_copies[0].wait()
    project(0, lambda p: og_ref[:, pl.ds(p * wide, wide)], True)

    for p in range(PIECES):
        for n, a in enumerate(across):
            forward_copy(a, p, n).wait_recv()
            forward_copy(a, p, n).start()

    for p in range(PIECES):
        forward_copy(mate, p, 0).wait_recv()
    w_copies[1].wait()
    project(1, lambda p: ogb[mate, p], False)

    for n, a in enumerate(across):
        w_copies[2 + n].wait()
        project(2 + n, lambda p, a=a: ogb[a, p], False)
    for n, a in enumerate(across_mate):
        for p in range(PIECES):
            forward_copy(a, p, n).wait_recv()
        w_copies[2 + len(across) + n].wait()
        project(2 + len(across) + n, lambda p, a=a: ogb[a, p], False)

    q_in.wait()

    def g_copy(i):
        return pltpu.make_async_remote_copy(
            src_ref=g.at[i], dst_ref=gn.at[i], send_sem=g_send.at[i], recv_sem=g_recv.at[i],
            device_id=(lax.rem(me + n_ctx - 1, n_ctx), tp), device_id_type=MESH,
        )

    @pl.loop(0, tiles)
    def _(i):
        cols = pl.ds(pl.multiple_of(i * LANES, LANES), LANES)
        m = mg[:, cols]
        g[i] = (m * q_ref[:, cols].astype(jnp.float32)).astype(jnp.bfloat16)

        @pl.when(me > 0)
        def _():
            g_copy(i).start()

    flip = jnp.where(row + col == rows - 1, 1.0, 0.0).astype(jnp.bfloat16)

    def upside_down(block):
        return jnp.dot(flip, block, preferred_element_type=jnp.float32).astype(jnp.bfloat16)

    @pl.when(me > 0)
    def _():
        x_copy.wait_recv()

    @pl.when(me == 0)
    def _():
        xp[...] = jnp.zeros_like(xp)

    @pl.loop(0, tiles, unroll=4)
    def _(i):
        gt = g[i]
        far = lax.dot_general(by_group(upside_down(xp[i])), gt, NT, preferred_element_type=jnp.float32)
        near = lax.dot_general(by_group(upside_down(x[i])), gt, NT, preferred_element_type=jnp.float32)
        for j in range(per_tile):
            at = slice(j * rows, (j + 1) * rows)
            pairs = jnp.where(col + row >= rows - 1, near[at], far[at])
            turned = pltpu.roll(pairs, 0, 1, stride=1, stride_axis=0)
            part[i, pl.ds(j, 1), :] = jnp.sum(turned, axis=0, keepdims=True)
        part[i, pl.ds(0, per_tile), :] = pltpu.roll(part[i, pl.ds(0, per_tile), :], 1, 1)
        both = gt.astype(jnp.float32) * x[i].astype(jnp.float32)
        part[i, pl.ds(per_tile, 8), :] = jnp.sum(both.reshape(rows // 8, 8, LANES), axis=0)

    def rs_copy(i):
        return pltpu.make_async_remote_copy(
            src_ref=part.at[i], dst_ref=rsb.at[me], send_sem=rs_send.at[i], recv_sem=rs_recv.at[me],
            device_id=(i * step, tp), device_id_type=MESH,
        )

    def rs_arrival(d):
        source = lax.rem(me + d, n_ctx)
        return source, pltpu.make_async_remote_copy(
            src_ref=part.at[0], dst_ref=rsb.at[source], send_sem=rs_send.at[0], recv_sem=rs_recv.at[source],
            device_id=(source, tp), device_id_type=MESH,
        )

    mine = me // step
    owner = lax.rem(me, step) == 0

    @pl.loop(0, tiles)
    def _(i):
        @pl.when(i * step != me)
        def _():
            rs_copy(i).start()

    s_in.wait()

    @pl.loop(0, tiles, unroll=4)
    def _(i):
        cols = pl.ds(pl.multiple_of(i * LANES, LANES), LANES)
        y = jnp.dot(a1[i], by_group(xp[i]), preferred_element_type=jnp.float32)
        y += jnp.dot(b1[i], by_group(x[i]), preferred_element_type=jnp.float32)
        y += s_ref[:, cols] * x[i].astype(jnp.float32)
        qg_ref[:, cols] = (mg[:, cols] * y).astype(jnp.bfloat16)

    @pl.loop(0, tiles, unroll=4)
    def _(i):
        cols = pl.ds(pl.multiple_of(i * LANES, LANES), LANES)
        z = jnp.dot(b2[i], by_group(g[i]), preferred_element_type=jnp.float32)
        mg[:, cols] = z + s_ref[:, cols] * g[i].astype(jnp.float32)

    def ag_copy(d):
        return pltpu.make_async_remote_copy(
            src_ref=red.at[mine], dst_ref=red.at[mine], send_sem=ag_send.at[d], recv_sem=ag_recv.at[mine],
            device_id=(lax.rem(me + d, n_ctx), tp), device_id_type=MESH,
        )

    def ag_arrival(i):
        return pltpu.make_async_remote_copy(
            src_ref=red.at[i], dst_ref=red.at[i], send_sem=ag_send.at[0], recv_sem=ag_recv.at[i],
            device_id=(i * step, tp), device_id_type=MESH,
        )

    @pl.when(owner)
    def _():
        def gather(d, total):
            source, arrival = rs_arrival(d)
            arrival.wait_recv()
            return total + rsb[source]

        red[mine] = lax.fori_loop(1, n_ctx, gather, part[mine])

        @pl.loop(1, n_ctx)
        def _(d):
            ag_copy(d).start()

    @pl.loop(0, tiles)
    def _(i):
        cols = pl.ds(pl.multiple_of(i * LANES, LANES), LANES)

        @pl.when(me < n_ctx - 1)
        def _():
            g_copy(i).wait_recv()
            mg[:, cols] += jnp.dot(a2[i], by_group(gn[i]), preferred_element_type=jnp.float32)

        z = mg[:, cols]
        kg_ref[:, cols] = (z * v_ref[:, cols].astype(jnp.float32)).astype(jnp.bfloat16)
        vg_ref[:, cols] = (z * k_ref[:, cols].astype(jnp.float32)).astype(jnp.bfloat16)

    for i in range(tiles):
        @pl.when(i * step != me)
        def _():
            ag_arrival(i).wait_recv()

        fg_ref[pl.ds(i * per_tile, per_tile), :] = red[i, pl.ds(0, per_tile), :]
        sg_ref[:, pl.ds(i * LANES, LANES)] = jnp.sum(red[i, pl.ds(per_tile, 8), :], axis=0, keepdims=True)

    for p in range(PIECES):
        for n, peer in enumerate(direct):
            og_copy(p, n, peer).wait_send()
        for n, a in enumerate(across):
            forward_copy(a, p, n).wait_send()

    @pl.when(me < n_ctx - 1)
    def _():
        x_copy.wait_send()

    @pl.when(me > 0)
    def _():
        @pl.loop(0, tiles)
        def _(i):
            g_copy(i).wait_send()

    @pl.loop(0, tiles)
    def _(i):
        @pl.when(i * step != me)
        def _():
            rs_copy(i).wait_send()

    @pl.when(owner)
    def _():
        @pl.loop(1, n_ctx)
        def _(d):
            ag_copy(d).wait_send()


def write_out(*refs):
    held, sem = refs[10:15], refs[15]
    ins = [pltpu.make_async_copy(refs[n], held[n], sem.at[0, n]) for n in range(5)]
    outs = [pltpu.make_async_copy(held[n], refs[5 + n], sem.at[1, n]) for n in range(5)]
    for copy in ins:
        copy.start()
    for n in range(5):
        ins[n].wait()
        outs[n].start()
    for copy in outs:
        copy.wait()


def on_device(n_ctx, n_tp, q, k, v, filters, skip_gain, out_grad, w_out):
    rows, channels = q.shape
    tiles = channels // LANES
    groups = filters.shape[0]
    block = (groups // tiles) + 8
    vmem = pl.BlockSpec(memory_space=pltpu.VMEM)
    bf, fl = jnp.bfloat16, jnp.float32
    dma = pltpu.SemaphoreType.DMA
    table = pltpu.VMEM((tiles, rows, (groups // tiles) * LANES), bf)
    slab = pltpu.VMEM((tiles, rows, LANES), bf)
    out = pl.pallas_call(
        functools.partial(kernel, n_ctx, n_tp),
        out_shape=(
            jax.ShapeDtypeStruct((rows, channels), bf),
            jax.ShapeDtypeStruct((rows, channels), bf),
            jax.ShapeDtypeStruct((rows, channels), bf),
            jax.ShapeDtypeStruct(filters.shape, fl),
            jax.ShapeDtypeStruct((1, channels), fl),
        ),
        in_specs=[pl.BlockSpec(memory_space=pltpu.HBM)] * 7,
        out_specs=(vmem,) * 5,
        scratch_shapes=[
            pltpu.VMEM((rows, channels), bf),
            pltpu.VMEM((rows, channels), bf),
            pltpu.VMEM((rows, channels), bf),
            pltpu.VMEM(filters.shape, fl),
            pltpu.VMEM((1, channels), fl),
            pltpu.VMEM((rows, channels), bf),
            dma((6,)),
            pltpu.VMEM((n_tp, channels, channels), bf),
            pltpu.VMEM((n_tp, PIECES, rows, channels // PIECES), bf),
            slab, slab, slab, slab,
            table, table, table, table,
            pltpu.VMEM((rows, channels), fl),
            pltpu.VMEM((tiles, block, LANES), fl),
            pltpu.VMEM((n_ctx, block, LANES), fl),
            pltpu.VMEM((tiles, block, LANES), fl),
            dma((n_tp,)),
            dma((n_tp // 2, PIECES)),
            dma((n_tp, PIECES)),
            dma((n_tp // 2, PIECES)),
            dma, dma,
            dma((tiles,)), dma((tiles,)),
            dma((tiles,)), dma((n_ctx,)),
            dma((n_ctx,)), dma((tiles,)),
        ],
        compiler_params=pltpu.CompilerParams(
            collective_id=0, has_side_effects=True, vmem_limit_bytes=56 * 1024 * 1024
        ),
        cost_estimate=pl.CostEstimate(
            flops=2 * rows * channels * channels * n_tp, bytes_accessed=2 * channels * channels * n_tp, transcendentals=0
        ),
    )(q, k, v, filters, skip_gain.reshape(1, channels), out_grad, w_out)
    out = pl.pallas_call(
        write_out,
        out_shape=[jax.ShapeDtypeStruct(o.shape, o.dtype) for o in out],
        in_specs=[pl.BlockSpec(memory_space=pltpu.HBM)] * 5,
        out_specs=[pl.BlockSpec(memory_space=pltpu.HBM)] * 5,
        scratch_shapes=[pltpu.VMEM(o.shape, o.dtype) for o in out] + [dma((2, 5))],
        compiler_params=pltpu.CompilerParams(vmem_limit_bytes=56 * 1024 * 1024),
    )(*out)
    return (out[0], out[1], out[2], out[3], out[4].reshape(channels))


def solution(mesh):
    n_ctx, n_tp = mesh.shape["ctx"], mesh.shape["tp"]
    return jax.shard_map(
        functools.partial(on_device, n_ctx, n_tp),
        mesh=mesh,
        in_specs=(
            P("ctx", "tp"),
            P("ctx", "tp"),
            P("ctx", "tp"),
            P("tp", None),
            P("tp"),
            P("ctx", "tp"),
            P("tp", None),
        ),
        out_specs=(P("ctx", "tp"), P("ctx", "tp"), P("ctx", "tp"), P("tp", None), P("tp")),
        check_vma=False,
    )
```

```python
import functools

import jax
import jax.numpy as jnp
from jax import lax
from jax.experimental import pallas as pl
from jax.experimental.pallas import tpu as pltpu
from jax.sharding import PartitionSpec as P

MESH = pl.DeviceIdType.MESH
LANES = 128
NT = (((1,), (1,)), ((), ()))
PIECES = 2


def kernel(
    n_ctx, n_tp,
    q_hbm, k_hbm, v_hbm, f_hbm, s_hbm, og_hbm, w_hbm,
    qg_ref, kg_ref, vg_ref, fg_ref, sg_ref,
    q_ref, k_ref, v_ref, f_ref, s_ref, og_ref, in_sem,
    wv, ogb, x, xp, g, gn, a1, b1, a2, b2, mg, part, rsb, red,
    w_sem, og_send, og_recv, fw_send, x_send, x_recv, g_send, g_recv,
    rs_send, rs_recv, ag_send, ag_recv,
):
    rows, channels = q_ref.shape
    tiles = channels // LANES
    per_tile = f_ref.shape[0] // tiles
    span = LANES // per_tile
    wide = channels // PIECES
    step = n_ctx // tiles
    me = lax.axis_index("ctx")
    tp = lax.axis_index("tp")
    mate = tp + 1 - 2 * lax.rem(tp, 2)
    across = [lax.rem(tp + 2 * d, n_tp) for d in range(1, n_tp // 2)]
    across_mate = [a + 1 - 2 * lax.rem(a, 2) for a in across]
    order = [tp, mate] + across + across_mate

    def bring(n, source, target):
        copy = pltpu.make_async_copy(source, target, in_sem.at[n])
        copy.start()
        return copy

    k_in = bring(0, k_hbm, k_ref)
    v_in = bring(1, v_hbm, v_ref)
    og_in = bring(2, og_hbm, og_ref)
    f_in = bring(3, f_hbm, f_ref)
    s_in = bring(4, s_hbm, s_ref)
    q_in = bring(5, q_hbm, q_ref)

    w_copies = []
    for n, slot in enumerate(order):
        copy = pltpu.make_async_copy(
            w_hbm.at[:, pl.ds(pl.multiple_of(slot * channels, channels), channels)], wv.at[n], w_sem.at[n]
        )
        copy.start()
        w_copies.append(copy)

    barrier = pltpu.get_barrier_semaphore()
    for peer in order[1:]:
        pl.semaphore_signal(barrier, inc=1, device_id=(me, peer), device_id_type=MESH)

    @pl.loop(1, n_ctx)
    def _(d):
        pl.semaphore_signal(barrier, inc=1, device_id=(lax.rem(me + d, n_ctx), tp), device_id_type=MESH)

    k_in.wait()
    v_in.wait()

    @pl.loop(0, tiles)
    def _(i):
        cols = pl.ds(pl.multiple_of(i * LANES, LANES), LANES)
        x[i] = (k_ref[:, cols].astype(jnp.float32) * v_ref[:, cols].astype(jnp.float32)).astype(jnp.bfloat16)

    og_in.wait()
    pl.semaphore_wait(barrier, n_tp - 1 + n_ctx - 1)

    def og_copy(p, n, peer):
        return pltpu.make_async_remote_copy(
            src_ref=og_ref.at[:, pl.ds(p * wide, wide)], dst_ref=ogb.at[tp, p],
            send_sem=og_send.at[n, p], recv_sem=og_recv.at[tp, p],
            device_id=(me, peer), device_id_type=MESH,
        )

    def forward_copy(slot, p, n):
        return pltpu.make_async_remote_copy(
            src_ref=ogb.at[slot, p], dst_ref=ogb.at[slot, p],
            send_sem=fw_send.at[n, p], recv_sem=og_recv.at[slot, p],
            device_id=(me, mate), device_id_type=MESH,
        )

    direct = across + [mate]
    for p in range(PIECES):
        for n, peer in enumerate(direct):
            og_copy(p, n, peer).start()

    x_copy = pltpu.make_async_remote_copy(
        src_ref=x, dst_ref=xp, send_sem=x_send, recv_sem=x_recv,
        device_id=(lax.rem(me + 1, n_ctx), tp), device_id_type=MESH,
    )

    @pl.when(me < n_ctx - 1)
    def _():
        x_copy.start()

    f_in.wait()
    row = lax.broadcasted_iota(jnp.int32, (rows, LANES), 0)
    col = lax.broadcasted_iota(jnp.int32, (rows, LANES), 1)
    mirror = jnp.where(lax.rem(row + col, LANES) == 0, 1.0, 0.0).astype(jnp.bfloat16)

    def spread(line):
        return pltpu.roll(jnp.broadcast_to(line, (rows, LANES)), 0, 1, stride=1, stride_axis=0)

    @pl.loop(0, tiles, unroll=4)
    def _(i):
        taps = f_ref[pl.ds(pl.multiple_of(i * per_tile, per_tile), per_tile), :]
        back = jnp.dot(taps.astype(jnp.bfloat16), mirror, preferred_element_type=jnp.float32)
        for j in range(per_tile):
            at = pl.ds(j * LANES, LANES)
            c1 = spread(back[j : j + 1])
            a1[i, :, at] = jnp.where(col > row, c1, 0.0).astype(jnp.bfloat16)
            b1[i, :, at] = jnp.where(col <= row, c1, 0.0).astype(jnp.bfloat16)
            c2 = spread(taps[j : j + 1])
            a2[i, :, at] = jnp.where(col < row, c2, 0.0).astype(jnp.bfloat16)
            b2[i, :, at] = jnp.where(col >= row, c2, 0.0).astype(jnp.bfloat16)

    lane = lax.broadcasted_iota(jnp.int32, (1, LANES), 1)
    masks = [
        jnp.where((lane >= j * span) & (lane < (j + 1) * span), 1.0, 0.0).astype(jnp.bfloat16)
        for j in range(per_tile)
    ]

    def by_group(block):
        return jnp.concatenate([block * m for m in masks], axis=0)

    def project(n, block_of, first):
        @pl.loop(0, tiles // 2, unroll=4)
        def _(i):
            chans = pl.ds(pl.multiple_of(i * 2 * LANES, 2 * LANES), 2 * LANES)
            total = None
            for p in range(PIECES):
                term = lax.dot_general(
                    block_of(p), wv[n, chans, pl.ds(p * wide, wide)], NT, preferred_element_type=jnp.float32
                )
                total = term if total is None else total + term
            if first:
                mg[:, chans] = total
            else:
                mg[:, chans] += total

    w_copies[0].wait()
    project(0, lambda p: og_ref[:, pl.ds(p * wide, wide)], True)

    for p in range(PIECES):
        forward_copy(mate, p, 0).wait_recv()
    w_copies[1].wait()
    project(1, lambda p: ogb[mate, p], False)

    @pl.when(me > 0)
    def _():
        x_copy.wait_recv()

    @pl.when(me == 0)
    def _():
        xp[...] = jnp.zeros_like(xp)

    for p in range(PIECES):
        for n, a in enumerate(across):
            forward_copy(a, p, n).wait_recv()
            forward_copy(a, p, n).start()

    for n, a in enumerate(across):
        w_copies[2 + n].wait()
        project(2 + n, lambda p, a=a: ogb[a, p], False)
    for n, a in enumerate(across_mate):
        for p in range(PIECES):
            forward_copy(a, p, n).wait_recv()
        w_copies[2 + len(across) + n].wait()
        project(2 + len(across) + n, lambda p, a=a: ogb[a, p], False)

    q_in.wait()

    def g_copy(i):
        return pltpu.make_async_remote_copy(
            src_ref=g.at[i], dst_ref=gn.at[i], send_sem=g_send.at[i], recv_sem=g_recv.at[i],
            device_id=(lax.rem(me + n_ctx - 1, n_ctx), tp), device_id_type=MESH,
        )

    @pl.loop(0, tiles)
    def _(i):
        cols = pl.ds(pl.multiple_of(i * LANES, LANES), LANES)
        m = mg[:, cols]
        g[i] = (m * q_ref[:, cols].astype(jnp.float32)).astype(jnp.bfloat16)

        @pl.when(me > 0)
        def _():
            g_copy(i).start()

    flip = jnp.where(row + col == rows - 1, 1.0, 0.0).astype(jnp.bfloat16)

    def upside_down(block):
        return jnp.dot(flip, block, preferred_element_type=jnp.float32).astype(jnp.bfloat16)

    @pl.loop(0, tiles, unroll=4)
    def _(i):
        gt = g[i]
        far = lax.dot_general(by_group(upside_down(xp[i])), gt, NT, preferred_element_type=jnp.float32)
        near = lax.dot_general(by_group(upside_down(x[i])), gt, NT, preferred_element_type=jnp.float32)
        for j in range(per_tile):
            at = slice(j * rows, (j + 1) * rows)
            pairs = jnp.where(col + row >= rows - 1, near[at], far[at])
            turned = pltpu.roll(pairs, 0, 1, stride=1, stride_axis=0)
            part[i, pl.ds(j, 1), :] = jnp.sum(turned, axis=0, keepdims=True)
        part[i, pl.ds(0, per_tile), :] = pltpu.roll(part[i, pl.ds(0, per_tile), :], 1, 1)
        both = gt.astype(jnp.float32) * x[i].astype(jnp.float32)
        part[i, pl.ds(per_tile, 8), :] = jnp.sum(both.reshape(rows // 8, 8, LANES), axis=0)

    def rs_copy(i):
        return pltpu.make_async_remote_copy(
            src_ref=part.at[i], dst_ref=rsb.at[me], send_sem=rs_send.at[i], recv_sem=rs_recv.at[me],
            device_id=(i * step, tp), device_id_type=MESH,
        )

    def rs_arrival(d):
        source = lax.rem(me + d, n_ctx)
        return source, pltpu.make_async_remote_copy(
            src_ref=part.at[0], dst_ref=rsb.at[source], send_sem=rs_send.at[0], recv_sem=rs_recv.at[source],
            device_id=(source, tp), device_id_type=MESH,
        )

    mine = me // step
    owner = lax.rem(me, step) == 0

    @pl.loop(0, tiles)
    def _(i):
        @pl.when(i * step != me)
        def _():
            rs_copy(i).start()

    s_in.wait()

    @pl.loop(0, tiles, unroll=4)
    def _(i):
        cols = pl.ds(pl.multiple_of(i * LANES, LANES), LANES)
        y = jnp.dot(a1[i], by_group(xp[i]), preferred_element_type=jnp.float32)
        y += jnp.dot(b1[i], by_group(x[i]), preferred_element_type=jnp.float32)
        y += s_ref[:, cols] * x[i].astype(jnp.float32)
        qg_ref[:, cols] = (mg[:, cols] * y).astype(jnp.bfloat16)

    @pl.loop(0, tiles, unroll=4)
    def _(i):
        cols = pl.ds(pl.multiple_of(i * LANES, LANES), LANES)
        z = jnp.dot(b2[i], by_group(g[i]), preferred_element_type=jnp.float32)
        mg[:, cols] = z + s_ref[:, cols] * g[i].astype(jnp.float32)

    def ag_copy(d):
        return pltpu.make_async_remote_copy(
            src_ref=red.at[mine], dst_ref=red.at[mine], send_sem=ag_send.at[d], recv_sem=ag_recv.at[mine],
            device_id=(lax.rem(me + d, n_ctx), tp), device_id_type=MESH,
        )

    def ag_arrival(i):
        return pltpu.make_async_remote_copy(
            src_ref=red.at[i], dst_ref=red.at[i], send_sem=ag_send.at[0], recv_sem=ag_recv.at[i],
            device_id=(i * step, tp), device_id_type=MESH,
        )

    @pl.when(owner)
    def _():
        def gather(d, total):
            source, arrival = rs_arrival(d)
            arrival.wait_recv()
            return total + rsb[source]

        red[mine] = lax.fori_loop(1, n_ctx, gather, part[mine])

        @pl.loop(1, n_ctx)
        def _(d):
            ag_copy(d).start()

    @pl.when(me < n_ctx - 1)
    def _():
        @pl.loop(0, tiles)
        def _(i):
            g_copy(i).wait_recv()

    @pl.when(me == n_ctx - 1)
    def _():
        gn[...] = jnp.zeros_like(gn)

    @pl.loop(0, tiles, unroll=4)
    def _(i):
        cols = pl.ds(pl.multiple_of(i * LANES, LANES), LANES)
        z = mg[:, cols] + jnp.dot(a2[i], by_group(gn[i]), preferred_element_type=jnp.float32)
        kg_ref[:, cols] = (z * v_ref[:, cols].astype(jnp.float32)).astype(jnp.bfloat16)
        vg_ref[:, cols] = (z * k_ref[:, cols].astype(jnp.float32)).astype(jnp.bfloat16)

    for i in range(tiles):
        @pl.when(i * step != me)
        def _():
            ag_arrival(i).wait_recv()

        fg_ref[pl.ds(i * per_tile, per_tile), :] = red[i, pl.ds(0, per_tile), :]
        sg_ref[:, pl.ds(i * LANES, LANES)] = jnp.sum(red[i, pl.ds(per_tile, 8), :], axis=0, keepdims=True)

    for p in range(PIECES):
        for n, peer in enumerate(direct):
            og_copy(p, n, peer).wait_send()
        for n, a in enumerate(across):
            forward_copy(a, p, n).wait_send()

    @pl.when(me < n_ctx - 1)
    def _():
        x_copy.wait_send()

    @pl.when(me > 0)
    def _():
        @pl.loop(0, tiles)
        def _(i):
            g_copy(i).wait_send()

    @pl.loop(0, tiles)
    def _(i):
        @pl.when(i * step != me)
        def _():
            rs_copy(i).wait_send()

    @pl.when(owner)
    def _():
        @pl.loop(1, n_ctx)
        def _(d):
            ag_copy(d).wait_send()


def write_out(*refs):
    held, sem = refs[10:15], refs[15]
    ins = [pltpu.make_async_copy(refs[n], held[n], sem.at[0, n]) for n in range(5)]
    outs = [pltpu.make_async_copy(held[n], refs[5 + n], sem.at[1, n]) for n in range(5)]
    for copy in ins:
        copy.start()
    for n in range(5):
        ins[n].wait()
        outs[n].start()
    for copy in outs:
        copy.wait()


def on_device(n_ctx, n_tp, q, k, v, filters, skip_gain, out_grad, w_out):
    rows, channels = q.shape
    tiles = channels // LANES
    groups = filters.shape[0]
    block = (groups // tiles) + 8
    vmem = pl.BlockSpec(memory_space=pltpu.VMEM)
    bf, fl = jnp.bfloat16, jnp.float32
    dma = pltpu.SemaphoreType.DMA
    table = pltpu.VMEM((tiles, rows, (groups // tiles) * LANES), bf)
    slab = pltpu.VMEM((tiles, rows, LANES), bf)
    out = pl.pallas_call(
        functools.partial(kernel, n_ctx, n_tp),
        out_shape=(
            jax.ShapeDtypeStruct((rows, channels), bf),
            jax.ShapeDtypeStruct((rows, channels), bf),
            jax.ShapeDtypeStruct((rows, channels), bf),
            jax.ShapeDtypeStruct(filters.shape, fl),
            jax.ShapeDtypeStruct((1, channels), fl),
        ),
        in_specs=[pl.BlockSpec(memory_space=pltpu.HBM)] * 7,
        out_specs=(vmem,) * 5,
        scratch_shapes=[
            pltpu.VMEM((rows, channels), bf),
            pltpu.VMEM((rows, channels), bf),
            pltpu.VMEM((rows, channels), bf),
            pltpu.VMEM(filters.shape, fl),
            pltpu.VMEM((1, channels), fl),
            pltpu.VMEM((rows, channels), bf),
            dma((6,)),
            pltpu.VMEM((n_tp, channels, channels), bf),
            pltpu.VMEM((n_tp, PIECES, rows, channels // PIECES), bf),
            slab, slab, slab, slab,
            table, table, table, table,
            pltpu.VMEM((rows, channels), fl),
            pltpu.VMEM((tiles, block, LANES), fl),
            pltpu.VMEM((n_ctx, block, LANES), fl),
            pltpu.VMEM((tiles, block, LANES), fl),
            dma((n_tp,)),
            dma((n_tp // 2, PIECES)),
            dma((n_tp, PIECES)),
            dma((n_tp // 2, PIECES)),
            dma, dma,
            dma((tiles,)), dma((tiles,)),
            dma((tiles,)), dma((n_ctx,)),
            dma((n_ctx,)), dma((tiles,)),
        ],
        compiler_params=pltpu.CompilerParams(
            collective_id=0, has_side_effects=True, vmem_limit_bytes=56 * 1024 * 1024
        ),
        cost_estimate=pl.CostEstimate(
            flops=2 * rows * channels * channels * n_tp, bytes_accessed=2 * channels * channels * n_tp, transcendentals=0
        ),
    )(q, k, v, filters, skip_gain.reshape(1, channels), out_grad, w_out)
    out = pl.pallas_call(
        write_out,
        out_shape=[jax.ShapeDtypeStruct(o.shape, o.dtype) for o in out],
        in_specs=[pl.BlockSpec(memory_space=pltpu.HBM)] * 5,
        out_specs=[pl.BlockSpec(memory_space=pltpu.HBM)] * 5,
        scratch_shapes=[pltpu.VMEM(o.shape, o.dtype) for o in out] + [dma((2, 5))],
        compiler_params=pltpu.CompilerParams(vmem_limit_bytes=56 * 1024 * 1024),
    )(*out)
    return (out[0], out[1], out[2], out[3], out[4].reshape(channels))


def solution(mesh):
    n_ctx, n_tp = mesh.shape["ctx"], mesh.shape["tp"]
    return jax.shard_map(
        functools.partial(on_device, n_ctx, n_tp),
        mesh=mesh,
        in_specs=(
            P("ctx", "tp"),
            P("ctx", "tp"),
            P("ctx", "tp"),
            P("tp", None),
            P("tp"),
            P("ctx", "tp"),
            P("tp", None),
        ),
        out_specs=(P("ctx", "tp"), P("ctx", "tp"), P("ctx", "tp"), P("tp", None), P("tp")),
        check_vma=False,
    )
```
